32 devices in a mesh: group: 2 (over x), wide: 16 (over z, y, core).
Axes of the slice: x: 2, y: 2, z: 4, core: 2. Of those that a mesh axis runs over, the one named last changes fastest.
Arguments:
- visibilities: float32 [6144, 2, 128], P(('group', 'wide')), parts along dimension 0, may hold values from -6 to 6
- offsets: float32 [6144, 2, 128], P(('group', 'wide')), parts along dimension 0, may hold values from 2 to 30
- vis_count: int32 [6144], P(('group', 'wide')), parts along dimension 0, may hold values from 1 to 128, 294912 in all
- owner: int32 [6144], P(('group', 'wide')), parts along dimension 0, may hold values from 0 to 15, as said below
- tile_row: int32 [6144], P(('group', 'wide')), parts along dimension 0, may hold values from 0 to 7
- tile_col: int32 [6144], P(('group', 'wide')), parts along dimension 0, may hold values from 0 to 127
Outputs:
- image: float32 [2, 8192, 4096], P(None, 'group', 'wide'), parts along dimension 1
The draws below stay inside these ranges and needn't reach their ends.
There are 2 independent parts, one for each index of `group`. The reference program is written for one: setup_inputs(seed, part) draws one part's arguments, and reference() takes and returns one part's arrays. A program takes and returns all parts, laid end to end along the dimension named above; each array names one. Nothing has to cross between parts.
Inputs may be any that keep to these rules, and one draw needn't show every extreme that they name: At most 36 subgrids of one device have the same owner; in every draw one owner receives exactly 36 subgrids from every device. `vis_count`: the live visibilities of a subgrid are the first ones of its slots; some subgrid has all 128 live; over each part along group the counts sum to 294912.
All inputs are finite; a program needn't handle non-finite values.
Results may differ from the reference program's by a relative error of at most 0.0003.
Values sent between devices are 32-bit elements; how exact they have to be, the bound alone decides.
No kernel may reach another device: no remote copies, remote signals or barrier semaphores. Data moves between devices by JAX's collectives and lax.ppermute only.
A program may use at most 128 MiB of HBM per device.

```python
import math
import jax
import jax.numpy as jnp
import numpy as np
from jax import lax

SUB = 32
VIS = 128
SUB_DEV = 192
GRID = 4096
OWNERS = 16
SUBGRIDS = 3072
CAP = 36
TROWS = 8
TCOLS = 128


def draw_owner(key, part):
    hot_key, bias_key, row_key = jax.random.split(key, 3)
    hottest = jax.random.randint(hot_key, (), 0, OWNERS)
    owner_bias = jax.random.randint(bias_key, (OWNERS,), 0, 4 * CAP)
    slot_index = jnp.arange(OWNERS * CAP).reshape(OWNERS, CAP)
    is_hot = jnp.arange(OWNERS)[:, None] == hottest
    rest_count = SUB_DEV - CAP

    def one_device(device_key):
        noise_key, order_key = jax.random.split(device_key)
        noise_draw = jax.random.randint(noise_key, (OWNERS, CAP), 0, 2 * CAP)
        scores = (owner_bias[:, None] + noise_draw) * (OWNERS * CAP) + slot_index
        scores = jnp.where(is_hot, -1, scores)
        chosen = lax.top_k(scores.reshape(-1), rest_count)[1] // CAP
        targets = jnp.concatenate([jnp.full((CAP,), hottest, jnp.int32), chosen.astype(jnp.int32)])
        return targets[jax.random.permutation(order_key, SUB_DEV)]
    device_keys = jax.random.split(row_key, OWNERS)
    return jax.vmap(one_device)(device_keys).reshape(-1).astype(jnp.int32)


def touch_ends(array, own_key, low, top_value):
    extent = array.shape
    spot = [jax.random.randint(jax.random.fold_in(own_key, axis), (), 0, extent[axis]) for axis in range(len(extent))]
    array = array.at[tuple(spot)].set(low)
    longest = extent.index(max(extent))
    spot[longest] = (spot[longest] + 1) % extent[longest]
    return array.at[tuple(spot)].set(top_value)


def block_scale(rng, extent, cuts, low, largest):
    def one(dim, blocks):
        steps = jax.random.uniform(jax.random.fold_in(jax.random.fold_in(rng, 6), dim), (blocks,), jnp.float32, low / len(cuts), largest / len(cuts))
        return jnp.repeat(jnp.exp(steps), extent[dim] // blocks).reshape((-1,) + (1,) * (len(extent) - dim - 1))

    level = one(*cuts[0])
    for cut in cuts[1:]:
        level = level * one(*cut)
    return level


def rank_table(amount, slope):
    weights = [(1 << 20) // math.isqrt(rank ** slope) + 1 for rank in range(1, amount + 1)]
    deviation = 1 + sum(weights) // (1 << 30)
    return np.cumsum(np.array([max(1, weight // deviation) for weight in weights]))


def ranked_ids(own_key, shape, amount, lean):
    grid = rank_table(amount, lean)
    lot = jax.random.randint(jax.random.fold_in(own_key, 1), shape, 0, int(grid[amount - 1]))
    standing = jnp.searchsorted(jnp.asarray(grid, jnp.int32), lot, side="right")
    return jax.random.permutation(jax.random.fold_in(own_key, 2), amount)[standing].astype(jnp.int32)


def length_profile(number_of, total, most, skew):
    portions = [(1 << 20) // math.isqrt(standing ** skew) + 1 for standing in range(2, number_of + 1)]
    rest, holding = total - most - (number_of - 1), [1] * (number_of - 1)
    while rest > 0:
        candidates = [i for i in range(number_of - 1) if holding[i] < most]
        pool, budget = sum([portions[i] for i in candidates]), rest
        for i in candidates:
            more = min(most - holding[i], max(1, budget * portions[i] // pool), rest)
            holding[i] = holding[i] + more
            rest = rest - more
    return np.array([most] + holding)


def uneven(key, amount, total, reach, slope):
    if amount == 2:
        one = jax.random.randint(key, (), max(1, total - reach), min(reach, total - 1) + 1)
        return jnp.stack([one, total - one])
    sizes = jnp.asarray(length_profile(amount, total, reach, slope), jnp.int32)
    pairs = (amount - 1) // 2
    source_of, receiver = sizes[1:1 + 2 * pairs:2], sizes[2:2 + 2 * pairs:2]
    room = jnp.minimum(source_of - 1, reach - receiver)
    moved = jax.random.randint(jax.random.fold_in(key, 1), (pairs,), 0, 1 << 20) % (room + 1)
    sizes = sizes.at[1:1 + 2 * pairs:2].set(source_of - moved).at[2:2 + 2 * pairs:2].set(receiver + moved)
    return sizes[jax.random.permutation(jax.random.fold_in(key, 2), amount)]


def normal_values(rng, dims, scale, reach, pieces=(), kind=jnp.bfloat16):
    values = jax.random.normal(rng, dims, jnp.float32) * scale
    if len(pieces) > 0:
        values = block_scale(rng, dims, pieces, -0.22, 0.18) * values
    return jnp.clip(values, min=-reach, max=reach).astype(kind)


def setup_inputs(seed: int = 0, part: int = 0) -> dict:
    key_list = jax.random.split(jax.random.key(seed), 7)
    part_keys = jax.random.split(jax.random.fold_in(key_list[6], part), 7)
    return {
        "visibilities": normal_values(part_keys[0], (SUBGRIDS, 2, VIS), 1.0, 6.0, ((0, 16),), jnp.float32),
        "offsets": jnp.clip(2.0 + 28.0 * jax.random.uniform(part_keys[1], (SUBGRIDS, 2, VIS), jnp.float32) ** block_scale(part_keys[1], (SUBGRIDS, 2, VIS), ((0, 16),), -0.2, 0.2), 2.0, 30.0),
        "vis_count": uneven(part_keys[2], SUBGRIDS, 3 * SUBGRIDS * VIS // 4, VIS, 1).astype(jnp.int32),
        "owner": draw_owner(jax.random.fold_in(jax.random.fold_in(key_list[6], part), 71), part),
        "tile_row": touch_ends(jax.random.randint(part_keys[4], (SUBGRIDS,), 0, TROWS), jax.random.fold_in(part_keys[4], 1), 0, TROWS - 1).astype(jnp.int32),
        "tile_col": touch_ends(ranked_ids(part_keys[5], (SUBGRIDS,), TCOLS, 2), jax.random.fold_in(part_keys[5], 3), 0, TCOLS - 1).astype(jnp.int32),
    }


highest = lax.Precision.HIGHEST

def cplx_einsum(pattern, left_real, left_imag, right_real, right_imag):

    def single(first, second):
        return jnp.einsum(pattern, first, second, precision=highest)
    return (single(left_real, right_real) - single(left_imag, right_imag), single(left_real, right_imag) + single(left_imag, right_real))

def subgrid_pixels(samples, counts):
    position = (jnp.arange(SUB, dtype=jnp.float32) - SUB // 2) / SUB
    live_mask = jnp.where(jnp.arange(VIS)[None, :] < counts[:, None], 1.0 / math.sqrt(VIS), 0.0)
    vis_real = samples[:, 0] * live_mask
    vis_imag = samples[:, 1] * live_mask
    angle_u = 2.0 * math.pi * samples[:, 2, :, None] * position
    angle_v = 2.0 * math.pi * samples[:, 3, :, None] * position
    cos_u, sin_u = (jnp.cos(angle_u), jnp.sin(angle_u))
    cos_v, sin_v = (jnp.cos(angle_v), jnp.sin(angle_v))
    weight_real = vis_real[:, :, None] * cos_u - vis_imag[:, :, None] * sin_u
    weight_imag = vis_real[:, :, None] * sin_u + vis_imag[:, :, None] * cos_u
    return cplx_einsum('nki,nkj->nij', weight_real, weight_imag, cos_v, sin_v)

def reference(visibilities, offsets, vis_count, owner, tile_row, tile_col):
    samples = jnp.concatenate([visibilities, offsets], axis=1).reshape(OWNERS, SUB_DEV, 4, VIS)
    counts = vis_count.reshape(OWNERS, SUB_DEV)

    def block_spectra(block_args):
        block_samples, block_counts = block_args
        pixel_real, pixel_imag = subgrid_pixels(block_samples, block_counts)
        spectra = jnp.fft.fft2(pixel_real + 1j * pixel_imag, norm='ortho')
        return jnp.stack([jnp.real(spectra), jnp.imag(spectra)], axis=1)
    spectra = lax.map(block_spectra, (samples, counts)).reshape(SUBGRIDS, 2, SUB, SUB)
    tile_index = (owner * TROWS + tile_row) * TCOLS + tile_col
    grid_tiles = jnp.zeros((GRID // SUB * TCOLS, 2, SUB, SUB), spectra.dtype).at[tile_index].add(spectra)
    grid_full = grid_tiles.reshape(GRID // SUB, TCOLS, 2, SUB, SUB).transpose(2, 0, 3, 1, 4).reshape(2, GRID, GRID)
    image = jnp.fft.fft2(grid_full[0] + 1j * grid_full[1], norm='ortho')
    return jnp.stack([jnp.real(image), jnp.imag(image)]).astype(jnp.float32)
```

```python
import functools
import math

import jax
import jax.numpy as jnp
import ml_dtypes
import numpy as np
from jax import lax
from jax.experimental import pallas as pl
from jax.experimental.pallas import tpu as pltpu
from jax.sharding import PartitionSpec as P

SUB = 32
GRID = 4096
LANES = 128
FB = GRID // LANES
BATCH = 8
CORES = 2

BF16 = jnp.bfloat16
F32 = jnp.float32


def split_np(table):
    table = table.astype(np.float32)
    high = table.astype(ml_dtypes.bfloat16)
    low = (table - high.astype(np.float32)).astype(ml_dtypes.bfloat16)
    return high, low


def embed(phase):
    angle = -2.0 * np.pi * (phase % GRID) / GRID
    real, imag = np.cos(angle), np.sin(angle)
    top = np.concatenate([real, -imag], axis=-1)
    bottom = np.concatenate([imag, real], axis=-1)
    return split_np(np.concatenate([top, bottom], axis=-2))


@functools.cache
def row_table():
    q = np.arange(FB)[:, None, None]
    m = np.arange(LANES)[None, :, None]
    t = np.arange(LANES)[None, None, :]
    return embed(m * (FB * t + q))


@functools.cache
def column_table():
    first = np.arange(FB)[:, None, None]
    outer = np.arange(LANES)[None, :, None]
    inner = np.arange(LANES)[None, None, :]
    return embed(inner * (first + FB * outer))


def even_fit(function, reach, degree):
    nodes = np.cos(np.pi * (np.arange(200) + 0.5) / 200)
    points = (nodes + 1.0) / 2.0 * reach * reach
    cheb = np.polynomial.chebyshev.Chebyshev.fit(
        points, function(np.sqrt(points)), degree, domain=[0.0, reach * reach]
    )
    return [float(c) for c in cheb.convert(kind=np.polynomial.Polynomial).coef]


SIN_FIT = even_fit(lambda x: np.sin(np.pi * x) / x, 0.5, 6)
COS_FIT = even_fit(lambda x: np.cos(np.pi * x), 0.5, 7)
PEAK_FIT = even_fit(lambda x: np.sin(np.pi * x) / np.tan(np.pi * x / SUB), 0.5, 6)


def horner(coefs, x):
    total = jnp.full_like(x, coefs[-1])
    for coef in coefs[-2::-1]:
        total = total * x + coef
    return total


def cot_table():
    grid = np.arange(SUB, dtype=np.float64)
    grid[0] = 1.0
    values = 1.0 / np.tan(np.pi * grid / SUB)
    values[0] = 1e30
    return np.tile(values.astype(np.float32)[:, None], (1, LANES))


def turn(value, k, n):
    real, imag = value
    k = k % n
    if k == 0:
        return value
    if 4 * k == n:
        return (imag, -real)
    if 2 * k == n:
        return (-real, -imag)
    if 8 * k == n:
        root = math.sqrt(0.5)
        return ((real + imag) * root, (imag - real) * root)
    if 8 * k == 3 * n:
        root = math.sqrt(0.5)
        return ((imag - real) * root, (real + imag) * -root)
    cos, sin = math.cos(2.0 * math.pi * k / n), -math.sin(2.0 * math.pi * k / n)
    return (real * cos - imag * sin, real * sin + imag * cos)


def fft_list(values):
    n = len(values)
    if n == 1:
        return values
    even, odd = fft_list(values[0::2]), fft_list(values[1::2])
    first, second = [], []
    for k in range(n // 2):
        turned = turn(odd[k], k, n)
        first.append((even[k][0] + turned[0], even[k][1] + turned[1]))
        second.append((even[k][0] - turned[0], even[k][1] - turned[1]))
    return first + second


def split(x):
    high = x.astype(BF16)
    return high, (x - high.astype(F32)).astype(BF16)


def dot(a, b):
    return lax.dot_general(a, b, (((1,), (0,)), ((), ())), preferred_element_type=F32)


def dot_nt(a, b):
    return lax.dot_general(a, b, (((1,), (1,)), ((), ())), preferred_element_type=F32)


def spectra_rows_kernel(
    blocks, outputs, bits, scale, info, order, coefs, *refs
):
    raws = refs[:blocks]
    cot_ref, high_hbm, low_hbm = refs[blocks : blocks + 3]
    outs = refs[blocks + 3 : blocks + 3 + CORES]
    raw, high, low, grid, sums, rows, prep, raw_sem, tab_sem = refs[blocks + 3 + CORES :]
    step = pl.program_id(0)
    per_block = raws[0].shape[0]
    raw_copies = [
        pltpu.make_async_copy(raws[i], raw.at[pl.ds(i * per_block, per_block)], raw_sem.at[i])
        for i in range(blocks)
    ]
    tab_copies = [
        pltpu.make_async_copy(high_hbm, high, tab_sem.at[0]),
        pltpu.make_async_copy(low_hbm, low, tab_sem.at[1]),
    ]

    @pl.when(step == 0)
    def _():
        for copy in raw_copies:
            copy.start()
        for copy in tab_copies:
            copy.start()

        def clear(i, _):
            grid[:, :, pl.ds(i * 128, 128), :] = jnp.zeros((2, 2, 128, LANES), F32)
            return 0

        lax.fori_loop(0, GRID // 128, clear, 0)
        for copy in raw_copies:
            copy.wait()

    me = info[0]
    start, end = info[1 + step], info[2 + step]
    last = order.shape[0] - 1
    cell = lax.broadcasted_iota(jnp.int32, (SUB, LANES), 0).astype(F32)
    lane_part = lax.broadcasted_iota(jnp.int32, (SUB, LANES), 1) // SUB
    sub_row = lax.broadcasted_iota(jnp.int32, (BATCH, LANES), 0)

    def batch(b, _):
        base = start + b * BATCH
        words = [order[jnp.minimum(base + j, last)] for j in range(BATCH)]
        for j in range(BATCH):
            item = words[j] & ((1 << bits) - 1)
            rows[4 * j : 4 * j + 4, :] = raw[pl.ds(4 * item, 4), :]
        factor = jnp.where(sub_row + base < end, scale, 0.0)
        re = rows[pl.ds(0, BATCH, stride=4), :] * factor
        im = rows[pl.ds(1, BATCH, stride=4), :] * factor
        for axis in range(2):
            u = rows[pl.ds(2 + axis, BATCH, stride=4), :]
            near = jnp.floor(u + 0.5)
            off = u - near
            sign = 1.0 - 2.0 * (near - 2.0 * jnp.floor(near * 0.5))
            wide = (u - SUB // 2) * (1.0 / SUB)
            wide2, off2 = wide * wide, off * off
            cot = -(wide * horner(SIN_FIT, wide2)) / horner(COS_FIT, wide2)
            sine = sign * (off * horner(SIN_FIT, off2))
            at = 8 * axis
            prep[at + 0] = cot
            prep[at + 1] = sine * cot
            prep[at + 2] = sine * (1.0 + cot * cot)
            prep[at + 3] = sign * horner(PEAK_FIT, off2)
            prep[at + 4] = near
            prep[at + 5] = sine
            if axis == 0:
                prep[6] = im * sine
                prep[7] = re * sine
        prep[14] = re
        prep[15] = im

        def table(axis, j):
            at = 8 * axis
            cot, alpha, beta, peak, near = [prep[at + i, j : j + 1, :] for i in range(5)]
            gap = cot_ref[...] - cot
            inv = pl.reciprocal(gap, approx=True)
            inv = inv * (2.0 - gap * inv)
            return jnp.where(cell == near, peak, alpha + beta * inv)

        found = []
        for j in range(BATCH):
            table_u, table_v = table(0, j), table(1, j)
            re_j, im_j = prep[14, j : j + 1, :], prep[15, j : j + 1, :]
            b_re = re_j * table_u + prep[6, j : j + 1, :]
            b_im = im_j * table_u - prep[7, j : j + 1, :]
            sine = jnp.broadcast_to(prep[13, j : j + 1, :], (16, LANES))
            a_high, a_low = split(jnp.concatenate([table_v, sine], axis=0))
            b_high, b_low = split(jnp.concatenate([b_re, b_im, b_im, -b_re], axis=0))
            product = dot_nt(
                jnp.concatenate([a_high, a_low, a_high], axis=1),
                jnp.concatenate([b_high, b_high, b_low], axis=1),
            )
            extra = pltpu.roll(product[SUB : SUB + 8], 64, 1)
            found.append(product[:SUB] + jnp.concatenate([extra] * (SUB // 8), axis=0))
        for j in range(BATCH):
            word = words[j]
            tile = (word >> bits) & (LANES - 1)
            part = (word >> (bits + 7)) & 3
            half = (word >> (bits + 9)) & 1
            mask = lane_part == part
            spot = pl.ds(pl.multiple_of(tile * SUB, SUB), SUB)
            grid[0, half, spot, :] += jnp.where(mask, pltpu.roll(found[j], part * SUB, 1), 0.0)
            moved = pltpu.roll(found[j], (part * SUB + 96) & 127, 1)
            grid[1, half, spot, :] += jnp.where(mask, moved, 0.0)
        return 0

    lax.fori_loop(0, (end - start + BATCH - 1) // BATCH, batch, 0)

    @pl.when(step == 0)
    def _():
        for copy in tab_copies:
            copy.wait()

    fine = FB // outputs
    zero = jnp.zeros((LANES, LANES), F32)
    sums[...] = jnp.zeros(sums.shape, F32)

    def transform(q0, _):
        parts = []
        for q1 in range(outputs):
            q = q0 + fine * q1
            at = pl.ds(q, LANES, stride=SUB)
            x = jnp.concatenate(
                [
                    jnp.concatenate([grid[c, 0, at, :], grid[c, 1, at, :]], axis=1)
                    for c in range(2)
                ],
                axis=0,
            )
            for c in range(2):
                for half in range(2):
                    grid[c, half, at, :] = zero
            x_high, x_low = split(x)
            f_high = high[q]
            y = dot(f_high, x_high) + dot(low[q], x_high) + dot(f_high, x_low)
            parts.append((y[:LANES], y[LANES:]))
        for j, (real, imag) in enumerate(fft_list(parts)):
            cos, sin = coefs[0, q0 * outputs + j], coefs[1, q0 * outputs + j]
            sums[j, 0] += real * cos - imag * sin
            sums[j, 1] += real * sin + imag * cos
        return 0

    lax.fori_loop(0, fine, transform, 0)
    share = outputs // CORES
    for slot in range(CORES):
        dest = (me + slot) % CORES
        for k in range(share):
            for c in range(2):
                for half in range(2):
                    outs[slot][half, c, k * LANES : (k + 1) * LANES, :] = sums[
                        dest * share + k, c, :, half * LANES : (half + 1) * LANES
                    ]


def spectra_rows(raws, info, order, coefs, columns, bits, scale):
    blocks = len(raws)
    outputs = CORES * columns // LANES
    per_device = FB // CORES
    steps = per_device // 2
    high, low = row_table()
    block = pl.BlockSpec((2, 2, columns, LANES), lambda i, *_: (i, 0, 0, 0))
    anywhere = pl.BlockSpec(memory_space=pl.ANY)
    raw_rows = blocks * raws[0].shape[0]
    return pl.pallas_call(
        functools.partial(spectra_rows_kernel, blocks, outputs, bits, scale),
        grid_spec=pltpu.PrefetchScalarGridSpec(
            num_scalar_prefetch=3,
            grid=(steps,),
            in_specs=[anywhere] * blocks
            + [pl.BlockSpec((SUB, LANES), lambda i, *_: (0, 0)), anywhere, anywhere],
            out_specs=[block] * CORES,
            scratch_shapes=[
                pltpu.VMEM((raw_rows, LANES), F32),
                pltpu.VMEM(high.shape, BF16),
                pltpu.VMEM(low.shape, BF16),
                pltpu.VMEM((2, 2, GRID, LANES), F32),
                pltpu.VMEM((outputs, 2, LANES, 2 * LANES), F32),
                pltpu.VMEM((4 * BATCH, LANES), F32),
                pltpu.VMEM((16, BATCH, LANES), F32),
                pltpu.SemaphoreType.DMA((blocks,)),
                pltpu.SemaphoreType.DMA((2,)),
            ],
        ),
        out_shape=[jax.ShapeDtypeStruct((per_device, 2, columns, LANES), F32)] * CORES,
        compiler_params=pltpu.CompilerParams(
            dimension_semantics=("arbitrary",), vmem_limit_bytes=56 * 1024 * 1024
        ),
        name="spectra_rows",
    )(info, order, coefs, *raws, jnp.asarray(cot_table()), jnp.asarray(high), jnp.asarray(low))


def columns_kernel(info, *refs):
    pieces = refs[:CORES]
    high_hbm, low_hbm, out, x, high, low, piece_sem, tab_sem = refs[CORES:]
    me = info[0]
    per_device, _, columns, _ = pieces[0].shape
    copies = [
        pltpu.make_async_copy(
            pieces[slot],
            x.at[pl.ds(((me + CORES - slot) % CORES) * per_device, per_device)],
            piece_sem.at[slot],
        )
        for slot in range(CORES)
    ]
    tab_copies = [
        pltpu.make_async_copy(high_hbm, high, tab_sem.at[0]),
        pltpu.make_async_copy(low_hbm, low, tab_sem.at[1]),
    ]
    for copy in copies + tab_copies:
        copy.start()
    for copy in copies:
        copy.wait()

    def butterflies(i, _):
        at = pl.ds(pl.multiple_of(i * 8, 8), 8)
        values = []
        for r in range(FB):
            slot = (r % CORES) * per_device + r // CORES
            values.append((x[slot, 0, at, :], x[slot, 1, at, :]))
        for r, (real, imag) in enumerate(fft_list(values)):
            x[r, 0, at, :] = real
            x[r, 1, at, :] = imag
        return 0

    lax.fori_loop(0, columns // 8, butterflies, 0)
    for copy in tab_copies:
        copy.wait()

    def transform(r, _):
        z_high, z_low = split(jnp.concatenate([x[r, 0], x[r, 1]], axis=1))
        f_high = high[r]
        y = dot_nt(f_high, z_high) + dot_nt(low[r], z_high) + dot_nt(f_high, z_low)
        at = pl.ds(r, LANES, stride=FB)
        for part in range(0, columns, LANES):
            out[0, part // LANES, at, :] = y[:LANES, part : part + LANES]
            out[1, part // LANES, at, :] = y[LANES:, part : part + LANES]
        return 0

    lax.fori_loop(0, FB, transform, 0)


def column_transform(pieces, info, columns):
    high, low = column_table()
    anywhere = pl.BlockSpec(memory_space=pl.ANY)

    def kernel(info, *refs):
        inputs, out_hbm = refs[: CORES + 2], refs[CORES + 2]
        out, x, high, low, piece_sem, tab_sem, out_sem = refs[CORES + 3 :]
        columns_kernel(info, *inputs, out, x, high, low, piece_sem, tab_sem)
        copies = [
            pltpu.make_async_copy(
                out.at[:, k], out_hbm.at[:, :, pl.ds(k * LANES, LANES)], out_sem.at[k]
            )
            for k in range(columns // LANES)
        ]
        for copy in copies:
            copy.start()
        for copy in copies:
            copy.wait()

    return pl.pallas_call(
        kernel,
        grid_spec=pltpu.PrefetchScalarGridSpec(
            num_scalar_prefetch=1,
            grid=(1,),
            in_specs=[anywhere] * (CORES + 2),
            out_specs=anywhere,
            scratch_shapes=[
                pltpu.VMEM((2, columns // LANES, GRID, LANES), F32),
                pltpu.VMEM((FB, 2, columns, LANES), F32),
                pltpu.VMEM(high.shape, BF16),
                pltpu.VMEM(low.shape, BF16),
                pltpu.SemaphoreType.DMA((CORES,)),
                pltpu.SemaphoreType.DMA((2,)),
                pltpu.SemaphoreType.DMA((columns // LANES,)),
            ],
        ),
        out_shape=jax.ShapeDtypeStruct((2, GRID, columns), F32),
        compiler_params=pltpu.CompilerParams(vmem_limit_bytes=56 * 1024 * 1024),
        name="column_transform",
    )(info, *pieces, jnp.asarray(high), jnp.asarray(low))


def chip_cycle(chips):
    return list(range(0, chips, 2)) + list(range(chips - 1, 0, -2))[: chips // 2]


def gather_blocks(block, size):
    chips = size // CORES
    cycle = chip_cycle(chips)
    ahead, back = [], []
    for at in range(chips):
        here, there = cycle[at], cycle[(at + 1) % chips]
        for core in range(CORES):
            ahead.append((CORES * here + core, CORES * there + core))
            back.append((CORES * there + core, CORES * here + core))
    swap = [(i, i ^ 1) for i in range(size)]
    found = {0: block}
    forth = other = block
    for k in range(1, chips // 2 + 1):
        forth = lax.ppermute(forth, "wide", ahead)
        found[k] = forth
        if 2 * k < chips:
            other = lax.ppermute(other, "wide", back)
            found[chips - k] = other
    own = jnp.concatenate([found[k] for k in range(chips)], axis=0)
    return [own, lax.ppermute(own, "wide", swap)]


def per_device(visibilities, offsets, vis_count, owner, tile_row, tile_col):
    size = lax.axis_size("wide")
    count, _, slots = visibilities.shape
    chips = size // CORES
    columns = GRID // size
    outputs = CORES * columns // LANES
    band_tiles = GRID // (SUB * size)
    place = lax.axis_index("wide")
    core, chip = place % CORES, place // CORES
    total = size * count
    bits = max(1, (total - 1).bit_length())

    live = (jnp.arange(slots)[None, :] < vis_count[:, None])[:, None, :]
    block = jnp.concatenate([jnp.where(live, visibilities, 0.0), offsets], axis=1)
    gathered = gather_blocks(block.reshape(count * 4, slots), size)

    row = owner * band_tiles + tile_row
    group, part = row // 4, row % 4
    key = (group % CORES) * (FB // CORES) + group // CORES
    word = (((key * 4 + part) * LANES + tile_col) << bits).astype(jnp.int32)
    words = lax.all_gather(word, "wide", axis=0, tiled=True)
    cycle = chip_cycle(chips)
    spot = np.zeros(chips, np.int32)
    spot[cycle] = np.arange(chips, dtype=np.int32)
    source = np.arange(size)
    distance = (jnp.asarray(spot)[chip] - spot[source // CORES]) % chips
    slot = ((source + core) % CORES) * chips + distance
    data_at = (slot[:, None] * count + jnp.arange(count)[None, :]).reshape(-1)
    order = lax.sort(words + data_at.astype(jnp.int32), is_stable=False)
    steps = FB // CORES // 2
    shift = bits + 7 + 2 + 1
    bounds = core * steps + jnp.arange(steps + 1)
    starts = jnp.sum((words[None, :] >> shift) < bounds[:, None], axis=1)
    info = jnp.concatenate([core[None], starts]).astype(jnp.int32)

    fine = FB // outputs
    phase = (
        jnp.arange(fine)[:, None] * (outputs * chip + jnp.arange(outputs)[None, :]) % FB
    ).astype(F32) * (-2.0 * math.pi / FB)
    coefs = jnp.stack([jnp.cos(phase).reshape(-1), jnp.sin(phase).reshape(-1)])

    scale = 1.0 / (math.sqrt(slots) * SUB * GRID)
    pieces = spectra_rows(gathered, info, order, coefs, columns, bits, scale)
    swap = [(i, i ^ 1) for i in range(size)]
    received = [pieces[0], lax.ppermute(pieces[1], "wide", swap)]
    return column_transform(received, info, columns)


def solution(mesh):
    placed = (
        P(("group", "wide"), None, None),
        P(("group", "wide"), None, None),
        P(("group", "wide")),
        P(("group", "wide")),
        P(("group", "wide")),
        P(("group", "wide")),
    )
    return jax.shard_map(
        per_device, mesh=mesh, in_specs=placed, out_specs=P(None, "group", "wide"), check_vma=False
    )
```

```python
import functools
import math

import jax
import jax.numpy as jnp
import ml_dtypes
import numpy as np
from jax import lax
from jax.experimental import pallas as pl
from jax.experimental.pallas import tpu as pltpu
from jax.sharding import PartitionSpec as P

SUB = 32
GRID = 4096
LANES = 128
FB = GRID // LANES
BATCH = 8
UNROLL = 4
CORES = 2

BF16 = jnp.bfloat16
F32 = jnp.float32


def split_np(table):
    table = table.astype(np.float32)
    high = table.astype(ml_dtypes.bfloat16)
    low = (table - high.astype(np.float32)).astype(ml_dtypes.bfloat16)
    return high, low


def embed(phase):
    angle = -2.0 * np.pi * (phase % GRID) / GRID
    real, imag = np.cos(angle), np.sin(angle)
    top = np.concatenate([real, -imag], axis=-1)
    bottom = np.concatenate([imag, real], axis=-1)
    return split_np(np.concatenate([top, bottom], axis=-2))


@functools.cache
def row_table(chips):
    count = LANES // chips
    first = np.arange(FB)[None, :, None, None]
    outer = np.arange(LANES).reshape(chips, 1, count, 1)
    inner = np.arange(LANES)[None, None, None, :]
    return np.concatenate(embed(inner * (first + FB * outer)), axis=2)


@functools.cache
def column_table():
    first = np.arange(FB)[:, None, None]
    outer = np.arange(LANES)[None, :, None]
    inner = np.arange(LANES)[None, None, :]
    return embed(inner * (first + FB * outer))


def even_fit(function, reach, degree):
    nodes = np.cos(np.pi * (np.arange(200) + 0.5) / 200)
    points = (nodes + 1.0) / 2.0 * reach * reach
    cheb = np.polynomial.chebyshev.Chebyshev.fit(
        points, function(np.sqrt(points)), degree, domain=[0.0, reach * reach]
    )
    return [float(c) for c in cheb.convert(kind=np.polynomial.Polynomial).coef]


SIN_FIT = even_fit(lambda x: np.sin(np.pi * x) / x, 0.5, 6)
COS_FIT = even_fit(lambda x: np.cos(np.pi * x), 0.5, 7)
PEAK_FIT = even_fit(lambda x: np.sin(np.pi * x) / np.tan(np.pi * x / SUB), 0.5, 6)


def horner(coefs, x):
    total = jnp.full_like(x, coefs[-1])
    for coef in coefs[-2::-1]:
        total = total * x + coef
    return total


def cot_table():
    grid = np.arange(SUB, dtype=np.float64)
    grid[0] = 1.0
    values = 1.0 / np.tan(np.pi * grid / SUB)
    values[0] = 1e30
    return np.tile(values.astype(np.float32)[:, None], (1, LANES))


def turn(value, k, n):
    real, imag = value
    k = k % n
    if k == 0:
        return value
    if 4 * k == n:
        return (imag, -real)
    if 2 * k == n:
        return (-real, -imag)
    if 8 * k == n:
        root = math.sqrt(0.5)
        return ((real + imag) * root, (imag - real) * root)
    if 8 * k == 3 * n:
        root = math.sqrt(0.5)
        return ((imag - real) * root, (real + imag) * -root)
    cos, sin = math.cos(2.0 * math.pi * k / n), -math.sin(2.0 * math.pi * k / n)
    return (real * cos - imag * sin, real * sin + imag * cos)


def fft_list(values):
    n = len(values)
    if n == 1:
        return values
    even, odd = fft_list(values[0::2]), fft_list(values[1::2])
    first, second = [], []
    for k in range(n // 2):
        turned = turn(odd[k], k, n)
        first.append((even[k][0] + turned[0], even[k][1] + turned[1]))
        second.append((even[k][0] - turned[0], even[k][1] - turned[1]))
    return first + second


def split(x):
    high = x.astype(BF16)
    return high, (x - high.astype(F32)).astype(BF16)


def dot(a, b):
    return lax.dot_general(a, b, (((1,), (0,)), ((), ())), preferred_element_type=F32)


def dot_nt(a, b):
    return lax.dot_general(a, b, (((1,), (1,)), ((), ())), preferred_element_type=F32)


def spectra_rows_kernel(blocks, bits, scale, info, order, *refs):
    raws = refs[:blocks]
    cot_ref, table_hbm = refs[blocks : blocks + 2]
    outs = refs[blocks + 2 : blocks + 2 + CORES]
    raw, table, grid, found, rows, prep, raw_sem, tab_sem = refs[blocks + 2 + CORES :]
    step = pl.program_id(0)
    per_block = raws[0].shape[0]
    raw_copies = [
        pltpu.make_async_copy(raws[i], raw.at[pl.ds(i * per_block, per_block)], raw_sem.at[i])
        for i in range(blocks)
    ]
    me, chip = info[0], info[1]
    tab_copy = pltpu.make_async_copy(table_hbm.at[chip], table, tab_sem.at[0])

    @pl.when(step == 0)
    def _():
        for copy in raw_copies:
            copy.start()
        tab_copy.start()

        def clear(i, _):
            grid[:, :, pl.ds(i * 128, 128), :] = jnp.zeros((2, 2, 128, LANES), F32)
            return 0

        lax.fori_loop(0, GRID // 128, clear, 0)
        for copy in raw_copies:
            copy.wait()
        tab_copy.wait()

    start, end = info[2 + step], info[3 + step]
    last = order.shape[0] - 1
    cell = lax.broadcasted_iota(jnp.int32, (SUB, LANES), 0).astype(F32)
    lane_part = lax.broadcasted_iota(jnp.int32, (SUB, LANES), 1) // SUB
    sub_row = lax.broadcasted_iota(jnp.int32, (BATCH, LANES), 0)

    def words_of(b):
        base = start + b * BATCH
        return [order[jnp.clip(base + j, 0, last)] for j in range(BATCH)]

    def prepare(b):
        base = start + b * BATCH
        words = words_of(b)
        for j in range(BATCH):
            item = words[j] & ((1 << bits) - 1)
            rows[4 * j : 4 * j + 4, :] = raw[pl.ds(4 * item, 4), :]
        factor = jnp.where(sub_row + base < end, scale, 0.0)
        re = rows[pl.ds(0, BATCH, stride=4), :] * factor
        im = rows[pl.ds(1, BATCH, stride=4), :] * factor
        values = {14: re, 15: im}
        for axis in range(2):
            u = rows[pl.ds(2 + axis, BATCH, stride=4), :]
            near = jnp.floor(u + 0.5)
            off = u - near
            sign = 1.0 - 2.0 * (near - 2.0 * jnp.floor(near * 0.5))
            wide = (u - SUB // 2) * (1.0 / SUB)
            wide2, off2 = wide * wide, off * off
            cot = -(wide * horner(SIN_FIT, wide2)) / horner(COS_FIT, wide2)
            sine = sign * (off * horner(SIN_FIT, off2))
            at = 8 * axis
            values[at + 0] = cot
            values[at + 1] = sine * cot
            values[at + 2] = sine * (1.0 + cot * cot)
            values[at + 3] = sign * horner(PEAK_FIT, off2)
            values[at + 4] = near
            values[at + 5] = sine
            if axis == 0:
                values[6] = im * sine
                values[7] = re * sine
        for at, value in values.items():
            prep[at] = value

    def dirichlet(axis, j):
        at = 8 * axis
        cot, alpha, beta, peak, near = [prep[at + i, j : j + 1, :] for i in range(5)]
        gap = cot_ref[...] - cot
        inv = pl.reciprocal(gap, approx=True)
        inv = inv * (2.0 - gap * inv)
        return jnp.where(cell == near, peak, alpha + beta * inv)

    def multiply():
        products = []
        for j in range(BATCH):
            table_u, table_v = dirichlet(0, j), dirichlet(1, j)
            re_j, im_j = prep[14, j : j + 1, :], prep[15, j : j + 1, :]
            b_re = re_j * table_u + prep[6, j : j + 1, :]
            b_im = im_j * table_u - prep[7, j : j + 1, :]
            sine = jnp.broadcast_to(prep[13, j : j + 1, :], (16, LANES))
            a_high, a_low = split(jnp.concatenate([table_v, sine], axis=0))
            b_high, b_low = split(jnp.concatenate([b_re, b_im, b_im, -b_re], axis=0))
            product = dot_nt(
                jnp.concatenate([a_high, a_low, a_high], axis=1),
                jnp.concatenate([b_high, b_high, b_low], axis=1),
            )
            extra = pltpu.roll(product[SUB : SUB + 8], 64, 1)
            products.append(product[:SUB] + jnp.concatenate([extra] * (SUB // 8), axis=0))
        return products

    def deposit(b):
        words = words_of(b)
        for j in range(BATCH):
            word = words[j]
            tile = (word >> bits) & (LANES - 1)
            part = (word >> (bits + 7)) & 3
            half = (word >> (bits + 9)) & 1
            mask = lane_part == part
            spot = pl.ds(pl.multiple_of(tile * SUB, SUB), SUB)
            value = found[j]
            grid[0, half, spot, :] += jnp.where(mask, pltpu.roll(value, part * SUB, 1), 0.0)
            moved = pltpu.roll(value, (part * SUB + 96) & 127, 1)
            grid[1, half, spot, :] += jnp.where(mask, moved, 0.0)

    found[...] = jnp.zeros(found.shape, F32)
    batches = (end - start + BATCH - 1) // BATCH
    prepare(0)

    def batch(b, _):
        deposit(b - 1)
        for j, product in enumerate(multiply()):
            found[j] = product
        prepare(b + 1)
        return 0

    lax.fori_loop(0, batches, batch, 0)
    deposit(batches - 1)

    def butterflies(i, _):
        for half in range(2):
            at = i * 8
            values = [
                tuple(grid[c, half, pl.ds(pl.multiple_of(r * LANES + at, 8), 8), :] for c in range(2))
                for r in range(FB)
            ]
            for r, value in enumerate(fft_list(values)):
                for c in range(2):
                    grid[c, half, pl.ds(pl.multiple_of(r * LANES + at, 8), 8), :] = value[c]
        return 0

    lax.fori_loop(0, LANES // 8, butterflies, 0)

    count = table.shape[1] // 4
    share = count // CORES
    zero = jnp.zeros((LANES, LANES), F32)

    def transform(r):
        at = pl.ds(pl.multiple_of(r * LANES, LANES), LANES)
        x = jnp.concatenate(
            [jnp.concatenate([grid[c, half, at, :] for half in range(2)], axis=1) for c in range(2)],
            axis=0,
        )
        x_high, x_low = split(x)
        f = table[r]
        y = dot(f, x_high)
        y = y[: 2 * count] + y[2 * count :] + dot(f[: 2 * count], x_low)
        return at, y

    def place(r, at, y):
        for c in range(2):
            for half in range(2):
                grid[c, half, at, :] = zero
        for c in range(2):
            shares = [
                y[c * count + k * share : c * count + (k + 1) * share] for k in range(CORES)
            ]
            for slot in range(CORES):
                value = shares[slot]
                for dest in range(CORES):
                    value = jnp.where((me + slot) % CORES == dest, shares[dest], value)
                for half in range(2):
                    outs[slot][half, c, pl.ds(r, share, stride=FB), :] = value[
                        :, half * LANES : (half + 1) * LANES
                    ]

    def several(i, _):
        done = [(i * UNROLL + k, *transform(i * UNROLL + k)) for k in range(UNROLL)]
        for item in done:
            place(*item)
        return 0

    lax.fori_loop(0, FB // UNROLL, several, 0)


def spectra_rows(raws, info, order, chips, columns, bits, scale):
    blocks = len(raws)
    per_device = FB // CORES
    steps = per_device // 2
    table = row_table(chips)
    block = pl.BlockSpec((2, 2, columns, LANES), lambda i, *_: (i, 0, 0, 0))
    anywhere = pl.BlockSpec(memory_space=pl.ANY)
    raw_rows = blocks * raws[0].shape[0]
    return pl.pallas_call(
        functools.partial(spectra_rows_kernel, blocks, bits, scale),
        grid_spec=pltpu.PrefetchScalarGridSpec(
            num_scalar_prefetch=2,
            grid=(steps,),
            in_specs=[anywhere] * blocks
            + [pl.BlockSpec((SUB, LANES), lambda i, *_: (0, 0)), anywhere],
            out_specs=[block] * CORES,
            scratch_shapes=[
                pltpu.VMEM((raw_rows, LANES), F32),
                pltpu.VMEM(table.shape[1:], BF16),
                pltpu.VMEM((2, 2, GRID, LANES), F32),
                pltpu.VMEM((BATCH, SUB, LANES), F32),
                pltpu.VMEM((4 * BATCH, LANES), F32),
                pltpu.VMEM((16, BATCH, LANES), F32),
                pltpu.SemaphoreType.DMA((blocks,)),
                pltpu.SemaphoreType.DMA((1,)),
            ],
        ),
        out_shape=[jax.ShapeDtypeStruct((per_device, 2, columns, LANES), F32)] * CORES,
        compiler_params=pltpu.CompilerParams(
            dimension_semantics=("arbitrary",), vmem_limit_bytes=56 * 1024 * 1024
        ),
        name="spectra_rows",
    )(info, order, *raws, jnp.asarray(cot_table()), jnp.asarray(table))


def columns_kernel(info, *refs):
    pieces = refs[:CORES]
    high_hbm, low_hbm, out, x, high, low, piece_sem, tab_sem = refs[CORES:]
    me = info[0]
    per_device, _, columns, _ = pieces[0].shape
    copies = [
        pltpu.make_async_copy(
            pieces[slot],
            x.at[pl.ds(((me + CORES - slot) % CORES) * per_device, per_device)],
            piece_sem.at[slot],
        )
        for slot in range(CORES)
    ]
    tab_copies = [
        pltpu.make_async_copy(high_hbm, high, tab_sem.at[0]),
        pltpu.make_async_copy(low_hbm, low, tab_sem.at[1]),
    ]
    for copy in copies + tab_copies:
        copy.start()
    for copy in copies:
        copy.wait()

    def butterflies(i, _):
        at = pl.ds(pl.multiple_of(i * 8, 8), 8)
        values = []
        for r in range(FB):
            slot = (r % CORES) * per_device + r // CORES
            values.append((x[slot, 0, at, :], x[slot, 1, at, :]))
        for r, (real, imag) in enumerate(fft_list(values)):
            x[r, 0, at, :] = real
            x[r, 1, at, :] = imag
        return 0

    lax.fori_loop(0, columns // 8, butterflies, 0)
    for copy in tab_copies:
        copy.wait()

    def transform(r):
        z_high, z_low = split(jnp.concatenate([x[r, 0], x[r, 1]], axis=1))
        f_high = high[r]
        return dot_nt(f_high, z_high) + dot_nt(low[r], z_high) + dot_nt(f_high, z_low)

    def several(i, _):
        done = [(i * UNROLL + k, transform(i * UNROLL + k)) for k in range(UNROLL)]
        for r, y in done:
            at = pl.ds(r, LANES, stride=FB)
            for part in range(0, columns, LANES):
                out[0, part // LANES, at, :] = y[:LANES, part : part + LANES]
                out[1, part // LANES, at, :] = y[LANES:, part : part + LANES]
        return 0

    lax.fori_loop(0, FB // UNROLL, several, 0)


def column_transform(pieces, info, columns):
    high, low = column_table()
    anywhere = pl.BlockSpec(memory_space=pl.ANY)

    def kernel(info, *refs):
        inputs, out_hbm = refs[: CORES + 2], refs[CORES + 2]
        out, x, high, low, piece_sem, tab_sem, out_sem = refs[CORES + 3 :]
        columns_kernel(info, *inputs, out, x, high, low, piece_sem, tab_sem)
        copies = [
            pltpu.make_async_copy(
                out.at[:, k], out_hbm.at[:, :, pl.ds(k * LANES, LANES)], out_sem.at[k]
            )
            for k in range(columns // LANES)
        ]
        for copy in copies:
            copy.start()
        for copy in copies:
            copy.wait()

    return pl.pallas_call(
        kernel,
        grid_spec=pltpu.PrefetchScalarGridSpec(
            num_scalar_prefetch=1,
            grid=(1,),
            in_specs=[anywhere] * (CORES + 2),
            out_specs=anywhere,
            scratch_shapes=[
                pltpu.VMEM((2, columns // LANES, GRID, LANES), F32),
                pltpu.VMEM((FB, 2, columns, LANES), F32),
                pltpu.VMEM(high.shape, BF16),
                pltpu.VMEM(low.shape, BF16),
                pltpu.SemaphoreType.DMA((CORES,)),
                pltpu.SemaphoreType.DMA((2,)),
                pltpu.SemaphoreType.DMA((columns // LANES,)),
            ],
        ),
        out_shape=jax.ShapeDtypeStruct((2, GRID, columns), F32),
        compiler_params=pltpu.CompilerParams(vmem_limit_bytes=56 * 1024 * 1024),
        name="column_transform",
    )(info, *pieces, jnp.asarray(high), jnp.asarray(low))


def chip_cycle(chips):
    return list(range(0, chips, 2)) + list(range(chips - 1, 0, -2))[: chips // 2]


def gather_blocks(block, size):
    chips = size // CORES
    cycle = chip_cycle(chips)
    ahead, back = [], []
    for at in range(chips):
        here, there = cycle[at], cycle[(at + 1) % chips]
        for core in range(CORES):
            ahead.append((CORES * here + core, CORES * there + core))
            back.append((CORES * there + core, CORES * here + core))
    swap = [(i, i ^ 1) for i in range(size)]
    found = {0: block}
    forth = other = block
    for k in range(1, chips // 2 + 1):
        forth = lax.ppermute(forth, "wide", ahead)
        found[k] = forth
        if 2 * k < chips:
            other = lax.ppermute(other, "wide", back)
            found[chips - k] = other
    own = jnp.concatenate([found[k] for k in range(chips)], axis=0)
    return [own, lax.ppermute(own, "wide", swap)]


def gather_words(words, size):
    if size & (size - 1):
        every = lax.all_gather(words, "wide", axis=0)
        return every[jnp.bitwise_xor(lax.axis_index("wide"), jnp.arange(size))].reshape(-1)
    hop = 1
    while hop < size:
        moved = lax.ppermute(words, "wide", [(i, i ^ hop) for i in range(size)])
        words = jnp.concatenate([words, moved])
        hop *= 2
    return words


def per_device(visibilities, offsets, vis_count, owner, tile_row, tile_col):
    size = lax.axis_size("wide")
    count, _, slots = visibilities.shape
    chips = size // CORES
    columns = GRID // size
    band_tiles = GRID // (SUB * size)
    place = lax.axis_index("wide")
    core, chip = place % CORES, place // CORES
    total = size * count
    bits = max(1, (total - 1).bit_length())

    live = (jnp.arange(slots)[None, :] < vis_count[:, None])[:, None, :]
    block = jnp.concatenate([jnp.where(live, visibilities, 0.0), offsets], axis=1)
    gathered = gather_blocks(block.reshape(count * 4, slots), size)

    row = owner * band_tiles + tile_row
    group, part = row // 4, row % 4
    key = (group % CORES) * (FB // CORES) + group // CORES
    word = (((key * 4 + part) * LANES + tile_col) << bits).astype(jnp.int32)
    words = gather_words(word, size)
    cycle = chip_cycle(chips)
    spot = np.zeros(chips, np.int32)
    spot[cycle] = np.arange(chips, dtype=np.int32)
    spot = jnp.asarray(spot)
    source = jnp.bitwise_xor(place, jnp.arange(size))
    distance = (spot[chip] - spot[source // CORES]) % chips
    slot = ((source + core) % CORES) * chips + distance
    data_at = (slot[:, None] * count + jnp.arange(count)[None, :]).reshape(-1)
    order = lax.sort(words + data_at.astype(jnp.int32), is_stable=False)
    steps = FB // CORES // 2
    shift = bits + 7 + 2 + 1
    bounds = core * steps + jnp.arange(steps + 1)
    starts = jnp.sum((words[None, :] >> shift) < bounds[:, None], axis=1)
    info = jnp.concatenate([core[None], chip[None], starts]).astype(jnp.int32)

    scale = 1.0 / (math.sqrt(slots) * SUB * GRID)
    pieces = spectra_rows(gathered, info, order, chips, columns, bits, scale)
    swap = [(i, i ^ 1) for i in range(size)]
    received = [pieces[0], lax.ppermute(pieces[1], "wide", swap)]
    return column_transform(received, info, columns)


def solution(mesh):
    placed = (
        P(("group", "wide"), None, None),
        P(("group", "wide"), None, None),
        P(("group", "wide")),
        P(("group", "wide")),
        P(("group", "wide")),
        P(("group", "wide")),
    )
    return jax.shard_map(
        per_device, mesh=mesh, in_specs=placed, out_specs=P(None, "group", "wide"), check_vma=False
    )
```

```python
import functools
import math

import jax
import jax.numpy as jnp
import ml_dtypes
import numpy as np
from jax import lax
from jax.experimental import pallas as pl
from jax.experimental.pallas import tpu as pltpu
from jax.sharding import PartitionSpec as P

SUB = 32
GRID = 4096
LANES = 128
FB = GRID // LANES
BATCH = 16
UNROLL = 8
RADIX = 8
REST = FB // RADIX
CORES = 2

BF16 = jnp.bfloat16
F32 = jnp.float32


def split_np(table):
    table = table.astype(np.float32)
    high = table.astype(ml_dtypes.bfloat16)
    low = (table - high.astype(np.float32)).astype(ml_dtypes.bfloat16)
    return high, low


def embed(phase):
    angle = -2.0 * np.pi * (phase % GRID) / GRID
    real, imag = np.cos(angle), np.sin(angle)
    top = np.concatenate([real, -imag], axis=-1)
    bottom = np.concatenate([imag, real], axis=-1)
    return split_np(np.concatenate([top, bottom], axis=-2))


@functools.cache
def row_base(chips):
    count = LANES // chips
    first = np.arange(RADIX)[:, None, None, None]
    output = first + RADIX * np.arange(REST * count)[None, :, None, None]
    inner = np.arange(REST * LANES).reshape(1, 1, REST, LANES)
    values = np.exp(-2j * np.pi * (output * inner % GRID) / GRID)

    def embedded(x):
        top = np.stack([x.real, -x.imag], axis=3)
        bottom = np.stack([x.imag, x.real], axis=3)
        full = np.concatenate([top, bottom], axis=1)
        return full.reshape(RADIX, 2 * REST * count, -1).astype(np.float32)

    return embedded(values), embedded(1j * values)


def row_table(chips, chip):
    plain, turned = row_base(chips)
    inner = np.arange(LANES) * (FB * (LANES // chips)) % GRID
    angle = (jnp.asarray(inner) * chip % GRID).astype(F32) * (-2.0 * math.pi / GRID)
    angle = jnp.tile(angle, 2 * REST)
    full = plain * jnp.cos(angle) + turned * jnp.sin(angle)
    high = lax.reduce_precision(full, 8, 7)
    return high.astype(BF16), (full - high).astype(BF16)


@functools.cache
def column_table():
    first = np.arange(FB)[:, None, None]
    outer = np.arange(LANES)[None, :, None]
    inner = np.arange(LANES)[None, None, :]
    return embed(inner * (first + FB * outer))


def even_fit(function, reach, degree):
    nodes = np.cos(np.pi * (np.arange(200) + 0.5) / 200)
    points = (nodes + 1.0) / 2.0 * reach * reach
    cheb = np.polynomial.chebyshev.Chebyshev.fit(
        points, function(np.sqrt(points)), degree, domain=[0.0, reach * reach]
    )
    return [float(c) for c in cheb.convert(kind=np.polynomial.Polynomial).coef]


SIN_FIT = even_fit(lambda x: np.sin(np.pi * x) / x, 0.5, 6)
COS_FIT = even_fit(lambda x: np.cos(np.pi * x), 0.5, 7)
PEAK_FIT = even_fit(lambda x: np.sin(np.pi * x) / np.tan(np.pi * x / SUB), 0.5, 6)


def horner(coefs, x):
    total = jnp.full_like(x, coefs[-1])
    for coef in coefs[-2::-1]:
        total = total * x + coef
    return total


def cot_table():
    grid = np.arange(SUB, dtype=np.float64)
    grid[0] = 1.0
    values = 1.0 / np.tan(np.pi * grid / SUB)
    values[0] = 1e30
    return np.tile(values.astype(np.float32)[:, None], (1, LANES))


def turn(value, k, n):
    real, imag = value
    k = k % n
    if k == 0:
        return value
    if 4 * k == n:
        return (imag, -real)
    if 2 * k == n:
        return (-real, -imag)
    if 8 * k == n:
        root = math.sqrt(0.5)
        return ((real + imag) * root, (imag - real) * root)
    if 8 * k == 3 * n:
        root = math.sqrt(0.5)
        return ((imag - real) * root, (real + imag) * -root)
    cos, sin = math.cos(2.0 * math.pi * k / n), -math.sin(2.0 * math.pi * k / n)
    return (real * cos - imag * sin, real * sin + imag * cos)


def fft_list(values):
    n = len(values)
    if n == 1:
        return values
    even, odd = fft_list(values[0::2]), fft_list(values[1::2])
    first, second = [], []
    for k in range(n // 2):
        turned = turn(odd[k], k, n)
        first.append((even[k][0] + turned[0], even[k][1] + turned[1]))
        second.append((even[k][0] - turned[0], even[k][1] - turned[1]))
    return first + second


def split(x):
    high = x.astype(BF16)
    return high, (x - high.astype(F32)).astype(BF16)


def dot(a, b):
    return lax.dot_general(a, b, (((1,), (0,)), ((), ())), preferred_element_type=F32)


def dot_nt(a, b):
    return lax.dot_general(a, b, (((1,), (1,)), ((), ())), preferred_element_type=F32)


def spectra_rows_kernel(blocks, bits, scale, info, order, *refs):
    raws = refs[:blocks]
    cot_ref, high_hbm, low_hbm = refs[blocks : blocks + 3]
    outs = refs[blocks + 3 : blocks + 3 + CORES]
    raw, table, grid, mixed_high, mixed_low, found, rows, prep, raw_sem, tab_sem = refs[blocks + 3 + CORES :]
    step = pl.program_id(0)
    raw_copies, at = [], 0
    for i in range(blocks):
        size = raws[i].shape[0]
        raw_copies.append(pltpu.make_async_copy(raws[i], raw.at[pl.ds(at, size)], raw_sem.at[i]))
        at += size
    me = info[0]
    both = high_hbm.shape[1]
    tab_copies = [
        pltpu.make_async_copy(high_hbm, table.at[:, pl.ds(0, both)], tab_sem.at[0]),
        pltpu.make_async_copy(low_hbm, table.at[:, pl.ds(both, both)], tab_sem.at[1]),
    ]

    @pl.when(step == 0)
    def _():
        for copy in raw_copies:
            copy.start()
        for copy in tab_copies:
            copy.start()

        def clear(i, _):
            grid[:, :, pl.ds(i * 128, 128), :] = jnp.zeros((2, 2, 128, LANES), F32)
            return 0

        lax.fori_loop(0, GRID // 128, clear, 0)
        for copy in raw_copies:
            copy.wait()

    start, end = info[1 + step], info[2 + step]
    last = order.shape[0] - 1
    cell = lax.broadcasted_iota(jnp.int32, (SUB, LANES), 0).astype(F32)
    lane_part = lax.broadcasted_iota(jnp.int32, (SUB, LANES), 1) // SUB
    sub_row = lax.broadcasted_iota(jnp.int32, (BATCH, LANES), 0)

    def words_of(b):
        base = start + b * BATCH
        return [order[jnp.clip(base + j, 0, last)] for j in range(BATCH)]

    def prepare(b):
        base = start + b * BATCH
        words = words_of(b)
        for j in range(BATCH):
            item = words[j] & ((1 << bits) - 1)
            rows[4 * j : 4 * j + 4, :] = raw[pl.ds(4 * item, 4), :]
        factor = jnp.where(sub_row + base < end, scale, 0.0)
        re = rows[pl.ds(0, BATCH, stride=4), :] * factor
        im = rows[pl.ds(1, BATCH, stride=4), :] * factor
        values = {14: re, 15: im}
        for axis in range(2):
            u = rows[pl.ds(2 + axis, BATCH, stride=4), :]
            near = jnp.floor(u + 0.5)
            off = u - near
            sign = 1.0 - 2.0 * (near - 2.0 * jnp.floor(near * 0.5))
            wide = (u - SUB // 2) * (1.0 / SUB)
            wide2, off2 = wide * wide, off * off
            cot = -(wide * horner(SIN_FIT, wide2)) / horner(COS_FIT, wide2)
            sine = sign * (off * horner(SIN_FIT, off2))
            at = 8 * axis
            values[at + 0] = cot
            values[at + 1] = sine * cot
            values[at + 2] = sine * (1.0 + cot * cot)
            values[at + 3] = sign * horner(PEAK_FIT, off2)
            values[at + 4] = near
            values[at + 5] = sine
            if axis == 0:
                values[6] = im * sine
                values[7] = re * sine
        for at, value in values.items():
            prep[at] = value

    def dirichlet(axis, j):
        at = 8 * axis
        cot, alpha, beta, peak, near = [prep[at + i, j : j + 1, :] for i in range(5)]
        gap = cot_ref[...] - cot
        inv = pl.reciprocal(gap, approx=True)
        return jnp.where(cell == near, peak, alpha + beta * inv)

    def multiply():
        products = []
        for j in range(BATCH):
            table_u, table_v = dirichlet(0, j), dirichlet(1, j)
            re_j, im_j = prep[14, j : j + 1, :], prep[15, j : j + 1, :]
            b_re = re_j * table_u + prep[6, j : j + 1, :]
            b_im = im_j * table_u - prep[7, j : j + 1, :]
            sine = jnp.broadcast_to(prep[13, j : j + 1, :], (16, LANES))
            a_high, a_low = split(jnp.concatenate([table_v, sine], axis=0))
            b_high, b_low = split(jnp.concatenate([b_re, b_im], axis=0))
            product = dot_nt(
                jnp.concatenate([a_high, a_low, a_high], axis=1),
                jnp.concatenate([b_high, b_high, b_low], axis=1),
            )
            product = jnp.concatenate([product, jnp.zeros_like(product)], axis=1)
            extra = product[SUB : SUB + 8]
            extra = jnp.where(lane_part[:8] == 0, pltpu.roll(extra, 96, 1), -pltpu.roll(extra, 32, 1))
            products.append(product[:SUB] + jnp.concatenate([extra] * (SUB // 8), axis=0))
        return products

    def deposit(b):
        words = words_of(b)
        for j in range(BATCH):
            word = words[j]
            tile = (word >> bits) & (LANES - 1)
            part = (word >> (bits + 7)) & 3
            half = (word >> (bits + 9)) & 1
            mask = lane_part == part
            spot = pl.ds(pl.multiple_of(tile * SUB, SUB), SUB)
            value = found[j]
            grid[0, half, spot, :] += jnp.where(mask, pltpu.roll(value, part * SUB, 1), 0.0)
            moved = pltpu.roll(value, (part * SUB + 96) & 127, 1)
            grid[1, half, spot, :] += jnp.where(mask, moved, 0.0)

    found[...] = jnp.zeros(found.shape, F32)
    batches = (end - start + BATCH - 1) // BATCH
    prepare(0)

    def batch(b, _):
        deposit(b - 1)
        for j, product in enumerate(multiply()):
            found[j] = product
        prepare(b + 1)
        return 0

    lax.fori_loop(0, batches, batch, 0)
    deposit(batches - 1)

    @pl.when(step == 0)
    def _():
        for copy in tab_copies:
            copy.wait()

    zero = jnp.zeros((16, LANES), F32)

    def butterflies(i, _):
        half, at = i % 2, pl.multiple_of(i // 2 * 16, 16)
        for b in range(REST):
            places = [
                pl.ds(pl.multiple_of((REST * a + b) * LANES + at, 16), 16) for a in range(RADIX)
            ]
            values = [tuple(grid[c, half, p, :] for c in range(2)) for p in places]
            for p in places:
                for c in range(2):
                    grid[c, half, p, :] = zero
            for r, value in enumerate(fft_list(values)):
                for c in range(2):
                    spot = pl.ds(pl.multiple_of((2 * b + c) * LANES + at, 16), 16)
                    mixed_high[r, half, spot, :], mixed_low[r, half, spot, :] = split(value[c])
        return 0

    lax.fori_loop(0, 2 * LANES // 16, butterflies, 0)

    outputs = table.shape[1] // 4
    share = outputs // CORES

    def transform(r):
        x_high = jnp.concatenate([mixed_high[r, 0], mixed_high[r, 1]], axis=1)
        x_low = jnp.concatenate([mixed_low[r, 0], mixed_low[r, 1]], axis=1)
        f = table[r]
        y = dot(f, x_high)
        return y[: 2 * outputs] + y[2 * outputs :] + dot(f[: 2 * outputs], x_low)

    def place(r, y):
        for c in range(2):
            shares = [
                y[c * outputs + k * share : c * outputs + (k + 1) * share] for k in range(CORES)
            ]
            for slot in range(CORES):
                value = shares[slot]
                for dest in range(CORES):
                    value = jnp.where((me + slot) % CORES == dest, shares[dest], value)
                for half in range(2):
                    outs[slot][half, c, pl.ds(r, share, stride=RADIX), :] = value[
                        :, half * LANES : (half + 1) * LANES
                    ]

    def several(i, _):
        done = [(2 * i + k, transform(2 * i + k)) for k in range(2)]
        for item in done:
            place(*item)
        return 0

    lax.fori_loop(0, RADIX // 2, several, 0)


def spectra_rows(raws, info, order, table, columns, bits, scale):
    blocks = len(raws)
    per_device = FB // CORES
    steps = per_device // 2
    block = pl.BlockSpec((2, 2, columns, LANES), lambda i, *_: (i, 0, 0, 0))
    anywhere = pl.BlockSpec(memory_space=pl.ANY)
    raw_rows = sum(x.shape[0] for x in raws)
    return pl.pallas_call(
        functools.partial(spectra_rows_kernel, blocks, bits, scale),
        grid_spec=pltpu.PrefetchScalarGridSpec(
            num_scalar_prefetch=2,
            grid=(steps,),
            in_specs=[anywhere] * blocks
            + [pl.BlockSpec((SUB, LANES), lambda i, *_: (0, 0)), anywhere, anywhere],
            out_specs=[block] * CORES,
            scratch_shapes=[
                pltpu.VMEM((raw_rows, LANES), F32),
                pltpu.VMEM((RADIX, 2 * table[0].shape[1], table[0].shape[2]), BF16),
                pltpu.VMEM((2, 2, GRID, LANES), F32),
                pltpu.VMEM((RADIX, 2, 2 * REST * LANES, LANES), BF16),
                pltpu.VMEM((RADIX, 2, 2 * REST * LANES, LANES), BF16),
                pltpu.VMEM((BATCH, SUB, LANES), F32),
                pltpu.VMEM((4 * BATCH, LANES), F32),
                pltpu.VMEM((16, BATCH, LANES), F32),
                pltpu.SemaphoreType.DMA((blocks,)),
                pltpu.SemaphoreType.DMA((2,)),
            ],
        ),
        out_shape=[jax.ShapeDtypeStruct((per_device, 2, columns, LANES), F32)] * CORES,
        compiler_params=pltpu.CompilerParams(
            dimension_semantics=("arbitrary",), vmem_limit_bytes=56 * 1024 * 1024
        ),
        name="spectra_rows",
    )(info, order, *raws, jnp.asarray(cot_table()), *table)


def columns_kernel(info, *refs):
    pieces = refs[:CORES]
    high_hbm, low_hbm, out, x, high, low, piece_sem, tab_sem = refs[CORES:]
    me = info[0]
    per_device, _, columns, _ = pieces[0].shape
    copies = [
        pltpu.make_async_copy(
            pieces[slot],
            x.at[pl.ds(((me + CORES - slot) % CORES) * per_device, per_device)],
            piece_sem.at[slot],
        )
        for slot in range(CORES)
    ]
    tab_copies = [
        pltpu.make_async_copy(high_hbm, high, tab_sem.at[0]),
        pltpu.make_async_copy(low_hbm, low, tab_sem.at[1]),
    ]
    for copy in copies + tab_copies:
        copy.start()
    for copy in copies:
        copy.wait()

    def butterflies(i, _):
        at = pl.ds(pl.multiple_of(i * 8, 8), 8)
        values = []
        for r in range(FB):
            slot = (r % CORES) * per_device + r // CORES
            values.append((x[slot, 0, at, :], x[slot, 1, at, :]))
        for r, (real, imag) in enumerate(fft_list(values)):
            x[r, 0, at, :] = real
            x[r, 1, at, :] = imag
        return 0

    lax.fori_loop(0, columns // 8, butterflies, 0)
    for copy in tab_copies:
        copy.wait()

    def transform(r):
        z_high, z_low = split(jnp.concatenate([x[r, 0], x[r, 1]], axis=1))
        f_high = high[r]
        return dot_nt(f_high, z_high) + dot_nt(low[r], z_high) + dot_nt(f_high, z_low)

    def several(i, _):
        done = [(i * UNROLL + k, transform(i * UNROLL + k)) for k in range(UNROLL)]
        for r, y in done:
            at = pl.ds(r, LANES, stride=FB)
            for part in range(0, columns, LANES):
                out[0, part // LANES, at, :] = y[:LANES, part : part + LANES]
                out[1, part // LANES, at, :] = y[LANES:, part : part + LANES]
        return 0

    lax.fori_loop(0, FB // UNROLL, several, 0)


def column_transform(pieces, info, columns):
    high, low = column_table()
    anywhere = pl.BlockSpec(memory_space=pl.ANY)

    def kernel(info, *refs):
        inputs, out_hbm = refs[: CORES + 2], refs[CORES + 2]
        out, x, high, low, piece_sem, tab_sem, out_sem = refs[CORES + 3 :]
        columns_kernel(info, *inputs, out, x, high, low, piece_sem, tab_sem)
        copies = [
            pltpu.make_async_copy(
                out.at[:, k], out_hbm.at[:, :, pl.ds(k * LANES, LANES)], out_sem.at[k]
            )
            for k in range(columns // LANES)
        ]
        for copy in copies:
            copy.start()
        for copy in copies:
            copy.wait()

    return pl.pallas_call(
        kernel,
        grid_spec=pltpu.PrefetchScalarGridSpec(
            num_scalar_prefetch=1,
            grid=(1,),
            in_specs=[anywhere] * (CORES + 2),
            out_specs=anywhere,
            scratch_shapes=[
                pltpu.VMEM((2, columns // LANES, GRID, LANES), F32),
                pltpu.VMEM((FB, 2, columns, LANES), F32),
                pltpu.VMEM(high.shape, BF16),
                pltpu.VMEM(low.shape, BF16),
                pltpu.SemaphoreType.DMA((CORES,)),
                pltpu.SemaphoreType.DMA((2,)),
                pltpu.SemaphoreType.DMA((columns // LANES,)),
            ],
        ),
        out_shape=jax.ShapeDtypeStruct((2, GRID, columns), F32),
        compiler_params=pltpu.CompilerParams(vmem_limit_bytes=56 * 1024 * 1024),
        name="column_transform",
    )(info, *pieces, jnp.asarray(high), jnp.asarray(low))


def chip_cycle(chips):
    return list(range(0, chips, 2)) + list(range(chips - 1, 0, -2))[: chips // 2]


def gather_all(block, size, half, beside):
    chips = size // CORES
    cycle = chip_cycle(chips)
    ahead, back = [], []
    for at in range(chips):
        here, there = cycle[at], cycle[(at + 1) % chips]
        for core in range(CORES):
            ahead.append((CORES * here + core, CORES * there + core))
            back.append((CORES * there + core, CORES * here + core))
    swap = [(i, i ^ 1) for i in range(size)]
    found = [[block]]
    forth = other = block
    for k in range(1, (chips + 2) // 2):
        if k == 3:
            forth, other, beside = lax.optimization_barrier((forth, other, beside))
        if 2 * k == chips:
            upper = lax.ppermute(forth[:half], "wide", ahead)
            lower = lax.ppermute(other[half:], "wide", back)
            found.append([upper, lower])
        else:
            forth = lax.ppermute(forth, "wide", ahead)
            other = lax.ppermute(other, "wide", back)
            found.append([forth, other])
    swapped = []
    for some in (found[:-2], found[-2:-1], found[-1:]):
        arrays = [x for each in some for x in each]
        if arrays:
            together = jnp.concatenate(arrays, axis=0) if len(arrays) > 1 else arrays[0]
            swapped.append(lax.ppermute(together, "wide", swap))
    return [x for each in found for x in each] + swapped, beside


def tags_of(arrays, rows, first, count):
    tag_rows = -(-count // LANES)
    parts, base = [], 0
    for array in arrays:
        end = base + array.shape[0]
        for at in range(-(-(base - first) // rows) * rows + first, end, rows):
            parts.append(array[at - base : at - base + tag_rows])
        base = end
    tags = jnp.stack(parts).reshape(len(parts), -1)[:, :count]
    return tags.astype(jnp.int32)


def per_device(visibilities, offsets, vis_count, owner, tile_row, tile_col):
    size = lax.axis_size("wide")
    count, _, slots = visibilities.shape
    chips = size // CORES
    columns = GRID // size
    band_tiles = GRID // (SUB * size)
    place = lax.axis_index("wide")
    core, chip = place % CORES, place // CORES
    first = 4 * count
    rows = first + 8 * -(-count // (8 * LANES))
    bits = (size * rows // 4 - 1).bit_length()

    live = (jnp.arange(slots)[None, :] < vis_count[:, None])[:, None, :]
    items = jnp.concatenate([jnp.where(live, visibilities, 0.0), offsets], axis=1)
    tiles = ((owner * band_tiles + tile_row) * LANES + tile_col).astype(F32)
    tiles = jnp.pad(tiles, (0, (rows - first) * LANES - count)).reshape(-1, LANES)
    block = jnp.concatenate([items.reshape(first, slots), tiles], axis=0)
    table = row_table(chips, chip)
    gathered, table = gather_all(block, size, rows // 16 * 8, table)

    tiles = tags_of(gathered, rows, first, count)
    group, part, tile_at = tiles // (4 * LANES), tiles // LANES % 4, tiles % LANES
    key = (group % CORES) * (FB // CORES) + group // CORES
    data_at = jnp.arange(size)[:, None] * (rows // 4) + jnp.arange(count)[None, :]
    word = (((key * 4 + part) * LANES + tile_at) << bits) + data_at
    order = lax.sort(word.reshape(-1).astype(jnp.int32), is_stable=False)
    steps = FB // CORES // 2
    shift = bits + 7 + 2 + 1
    bounds = core * steps + jnp.arange(steps + 1)
    starts = jnp.sum((order[None, :] >> shift) < bounds[:, None], axis=1)
    info = jnp.concatenate([core[None], starts]).astype(jnp.int32)

    scale = 1.0 / (math.sqrt(slots) * SUB * GRID)
    pieces = spectra_rows(gathered, info, order, table, columns, bits, scale)
    swap = [(i, i ^ 1) for i in range(size)]
    received = [pieces[0], lax.ppermute(pieces[1], "wide", swap)]
    return column_transform(received, info, columns)


def solution(mesh):
    placed = (
        P(("group", "wide"), None, None),
        P(("group", "wide"), None, None),
        P(("group", "wide")),
        P(("group", "wide")),
        P(("group", "wide")),
        P(("group", "wide")),
    )
    return jax.shard_map(
        per_device, mesh=mesh, in_specs=placed, out_specs=P(None, "group", "wide"), check_vma=False
    )
```

```python
import functools
import math

import jax
import jax.numpy as jnp
import ml_dtypes
import numpy as np
from jax import lax
from jax.experimental import pallas as pl
from jax.experimental.pallas import tpu as pltpu
from jax.sharding import PartitionSpec as P

SUB = 32
GRID = 4096
LANES = 128
FB = GRID // LANES
BATCH = 32
UNROLL = 8
RADIX = 8
REST = FB // RADIX
CORES = 2

BF16 = jnp.bfloat16
F32 = jnp.float32


def split_np(table):
    table = table.astype(np.float32)
    high = table.astype(ml_dtypes.bfloat16)
    low = (table - high.astype(np.float32)).astype(ml_dtypes.bfloat16)
    return high, low


def embed(phase):
    angle = -2.0 * np.pi * (phase % GRID) / GRID
    real, imag = np.cos(angle), np.sin(angle)
    top = np.concatenate([real, -imag], axis=-1)
    bottom = np.concatenate([imag, real], axis=-1)
    return split_np(np.concatenate([top, bottom], axis=-2))


@functools.cache
def row_table(chips):
    count = LANES // chips
    chip = np.arange(chips)[:, None, None, None, None]
    first = np.arange(RADIX)[None, :, None, None, None]
    output = np.arange(REST * count)[None, None, :, None, None] + REST * count * chip
    inner = np.arange(REST * LANES).reshape(1, 1, 1, REST, LANES)
    phase = (first + RADIX * output) * inner % GRID
    roots = np.exp(-2j * np.pi * np.arange(GRID) / GRID)
    real, imag = roots.real.astype(np.float32)[phase], roots.imag.astype(np.float32)[phase]
    top = np.stack([real, -imag], axis=4)
    bottom = np.stack([imag, real], axis=4)
    full = np.concatenate([top, bottom], axis=2)
    full = full.reshape(chips, RADIX, 2 * REST * count, -1)
    return np.concatenate(split_np(full), axis=2)


@functools.cache
def column_table():
    first = np.arange(FB)[:, None, None]
    outer = np.arange(LANES)[None, :, None]
    inner = np.arange(LANES)[None, None, :]
    return embed(inner * (first + FB * outer))


def even_fit(function, reach, degree):
    nodes = np.cos(np.pi * (np.arange(200) + 0.5) / 200)
    points = (nodes + 1.0) / 2.0 * reach * reach
    cheb = np.polynomial.chebyshev.Chebyshev.fit(
        points, function(np.sqrt(points)), degree, domain=[0.0, reach * reach]
    )
    return [float(c) for c in cheb.convert(kind=np.polynomial.Polynomial).coef]


SIN_FIT = even_fit(lambda x: np.sin(np.pi * x) / x, 0.5, 6)
COS_FIT = even_fit(lambda x: np.cos(np.pi * x), 0.5, 7)
PEAK_FIT = even_fit(lambda x: np.sin(np.pi * x) / np.tan(np.pi * x / SUB), 0.5, 6)


def horner(coefs, x):
    total = jnp.full_like(x, coefs[-1])
    for coef in coefs[-2::-1]:
        total = total * x + coef
    return total


def cot_table():
    grid = np.arange(SUB, dtype=np.float64)
    grid[0] = 1.0
    values = 1.0 / np.tan(np.pi * grid / SUB)
    values[0] = 1e30
    return np.tile(values.astype(np.float32)[:, None], (1, LANES))


def turn(value, k, n):
    real, imag = value
    k = k % n
    if k == 0:
        return value
    if 4 * k == n:
        return (imag, -real)
    if 2 * k == n:
        return (-real, -imag)
    if 8 * k == n:
        root = math.sqrt(0.5)
        return ((real + imag) * root, (imag - real) * root)
    if 8 * k == 3 * n:
        root = math.sqrt(0.5)
        return ((imag - real) * root, (real + imag) * -root)
    cos, sin = math.cos(2.0 * math.pi * k / n), -math.sin(2.0 * math.pi * k / n)
    return (real * cos - imag * sin, real * sin + imag * cos)


def fft_list(values):
    n = len(values)
    if n == 1:
        return values
    even, odd = fft_list(values[0::2]), fft_list(values[1::2])
    first, second = [], []
    for k in range(n // 2):
        turned = turn(odd[k], k, n)
        first.append((even[k][0] + turned[0], even[k][1] + turned[1]))
        second.append((even[k][0] - turned[0], even[k][1] - turned[1]))
    return first + second


def split(x):
    high = x.astype(BF16)
    return high, (x - high.astype(F32)).astype(BF16)


def dot(a, b):
    return lax.dot_general(a, b, (((1,), (0,)), ((), ())), preferred_element_type=F32)


def dot_nt(a, b):
    return lax.dot_general(a, b, (((1,), (1,)), ((), ())), preferred_element_type=F32)


def spectra_rows_kernel(blocks, bits, scale, info, order, *refs):
    raws = refs[:blocks]
    cot_ref, table_hbm = refs[blocks : blocks + 2]
    outs = refs[blocks + 2 : blocks + 2 + CORES]
    raw, table, grid, mixed_high, mixed_low, found, rows, prep, raw_sem, tab_sem = refs[blocks + 2 + CORES :]
    step = pl.program_id(0)
    raw_copies, at = [], 0
    for i in range(blocks):
        size = raws[i].shape[0]
        raw_copies.append(pltpu.make_async_copy(raws[i], raw.at[pl.ds(at, size)], raw_sem.at[i]))
        at += size
    me = info[0]
    tab_copy = pltpu.make_async_copy(table_hbm.at[info[1]], table, tab_sem.at[0])

    @pl.when(step == 0)
    def _():
        for copy in raw_copies:
            copy.start()
        tab_copy.start()

        def clear(i, _):
            grid[:, :, pl.ds(i * 128, 128), :] = jnp.zeros((2, 2, 128, LANES), F32)
            return 0

        lax.fori_loop(0, GRID // 128, clear, 0)
        for copy in raw_copies:
            copy.wait()

    start, end = info[2 + step], info[3 + step]
    last = order.shape[0] - 1
    cell = lax.broadcasted_iota(jnp.int32, (SUB, LANES), 0).astype(F32)
    lane_part = lax.broadcasted_iota(jnp.int32, (SUB, LANES), 1) // SUB
    sub_row = lax.broadcasted_iota(jnp.int32, (BATCH, LANES), 0)

    def words_of(b):
        base = start + b * BATCH
        return [order[jnp.clip(base + j, 0, last)] for j in range(BATCH)]

    def prepare(b):
        base = start + b * BATCH
        words = words_of(b)
        for j in range(BATCH):
            item = words[j] & ((1 << bits) - 1)
            rows[4 * j : 4 * j + 4, :] = raw[pl.ds(4 * item, 4), :]
        factor = jnp.where(sub_row + base < end, scale, 0.0)
        re = rows[pl.ds(0, BATCH, stride=4), :] * factor
        im = rows[pl.ds(1, BATCH, stride=4), :] * factor
        values = {14: re, 15: im}
        for axis in range(2):
            u = rows[pl.ds(2 + axis, BATCH, stride=4), :]
            near = jnp.floor(u + 0.5)
            off = u - near
            sign = 1.0 - 2.0 * (near - 2.0 * jnp.floor(near * 0.5))
            wide = (u - SUB // 2) * (1.0 / SUB)
            wide2, off2 = wide * wide, off * off
            cot = -(wide * horner(SIN_FIT, wide2)) / horner(COS_FIT, wide2)
            sine = sign * (off * horner(SIN_FIT, off2))
            at = 8 * axis
            values[at + 0] = cot
            values[at + 1] = sine * cot
            values[at + 2] = sine * (1.0 + cot * cot)
            values[at + 3] = sign * horner(PEAK_FIT, off2)
            values[at + 4] = near
            values[at + 5] = sine
            if axis == 0:
                values[6] = im * sine
                values[7] = re * sine
        for at, value in values.items():
            prep[at] = value

    def dirichlet(axis, j):
        at = 8 * axis
        cot, alpha, beta, peak, near = [prep[at + i, j : j + 1, :] for i in range(5)]
        gap = cot_ref[...] - cot
        inv = pl.reciprocal(gap, approx=True)
        return jnp.where(cell == near, peak, alpha + beta * inv)

    def multiply():
        products = []
        for j in range(BATCH):
            table_u, table_v = dirichlet(0, j), dirichlet(1, j)
            re_j, im_j = prep[14, j : j + 1, :], prep[15, j : j + 1, :]
            b_re = re_j * table_u + prep[6, j : j + 1, :]
            b_im = im_j * table_u - prep[7, j : j + 1, :]
            sine = jnp.broadcast_to(prep[13, j : j + 1, :], (16, LANES))
            a_high, a_low = split(jnp.concatenate([table_v, sine], axis=0))
            b_high, b_low = split(jnp.concatenate([b_re, b_im], axis=0))
            product = dot_nt(
                jnp.concatenate([a_high, a_low, a_high], axis=1),
                jnp.concatenate([b_high, b_high, b_low], axis=1),
            )
            product = jnp.concatenate([product, jnp.zeros_like(product)], axis=1)
            extra = product[SUB : SUB + 8]
            extra = jnp.where(lane_part[:8] == 0, pltpu.roll(extra, 96, 1), -pltpu.roll(extra, 32, 1))
            products.append(product[:SUB] + jnp.concatenate([extra] * (SUB // 8), axis=0))
        return products

    def deposit(b):
        words = words_of(b)
        for j in range(BATCH):
            word = words[j]
            tile = (word >> bits) & (LANES - 1)
            part = (word >> (bits + 7)) & 3
            half = (word >> (bits + 9)) & 1
            mask = lane_part == part
            spot = pl.ds(pl.multiple_of(tile * SUB, SUB), SUB)
            value = found[j]
            grid[0, half, spot, :] += jnp.where(mask, pltpu.roll(value, part * SUB, 1), 0.0)
            moved = pltpu.roll(value, (part * SUB + 96) & 127, 1)
            grid[1, half, spot, :] += jnp.where(mask, moved, 0.0)

    found[...] = jnp.zeros(found.shape, F32)
    batches = (end - start + BATCH - 1) // BATCH
    prepare(0)

    def batch(b, _):
        deposit(b - 1)
        for j, product in enumerate(multiply()):
            found[j] = product
        prepare(b + 1)
        return 0

    lax.fori_loop(0, batches, batch, 0)
    deposit(batches - 1)

    @pl.when(step == 0)
    def _():
        tab_copy.wait()

    zero = jnp.zeros((16, LANES), F32)

    def butterflies(i, _):
        half, at = i % 2, pl.multiple_of(i // 2 * 16, 16)
        for b in range(REST):
            places = [
                pl.ds(pl.multiple_of((REST * a + b) * LANES + at, 16), 16) for a in range(RADIX)
            ]
            values = [tuple(grid[c, half, p, :] for c in range(2)) for p in places]
            for p in places:
                for c in range(2):
                    grid[c, half, p, :] = zero
            for r, value in enumerate(fft_list(values)):
                for c in range(2):
                    spot = pl.ds(pl.multiple_of((2 * b + c) * LANES + at, 16), 16)
                    mixed_high[r, half, spot, :], mixed_low[r, half, spot, :] = split(value[c])
        return 0

    lax.fori_loop(0, 2 * LANES // 16, butterflies, 0)

    outputs = table.shape[1] // 4
    share = outputs // CORES

    def transform(r):
        x_high = jnp.concatenate([mixed_high[r, 0], mixed_high[r, 1]], axis=1)
        x_low = jnp.concatenate([mixed_low[r, 0], mixed_low[r, 1]], axis=1)
        f = table[r]
        y = dot(f, x_high)
        return y[: 2 * outputs] + y[2 * outputs :] + dot(f[: 2 * outputs], x_low)

    def place(r, y):
        for c in range(2):
            shares = [
                y[c * outputs + k * share : c * outputs + (k + 1) * share] for k in range(CORES)
            ]
            for slot in range(CORES):
                value = shares[slot]
                for dest in range(CORES):
                    value = jnp.where((me + slot) % CORES == dest, shares[dest], value)
                for half in range(2):
                    outs[slot][half, c, pl.ds(r, share, stride=RADIX), :] = value[
                        :, half * LANES : (half + 1) * LANES
                    ]

    def several(i, _):
        done = [(2 * i + k, transform(2 * i + k)) for k in range(2)]
        for item in done:
            place(*item)
        return 0

    lax.fori_loop(0, RADIX // 2, several, 0)


def spectra_rows(raws, info, order, chips, columns, bits, scale):
    blocks = len(raws)
    table = row_table(chips)
    per_device = FB // CORES
    steps = per_device // 2
    block = pl.BlockSpec((2, 2, columns, LANES), lambda i, *_: (i, 0, 0, 0))
    anywhere = pl.BlockSpec(memory_space=pl.ANY)
    raw_rows = sum(x.shape[0] for x in raws)
    return pl.pallas_call(
        functools.partial(spectra_rows_kernel, blocks, bits, scale),
        grid_spec=pltpu.PrefetchScalarGridSpec(
            num_scalar_prefetch=2,
            grid=(steps,),
            in_specs=[anywhere] * blocks
            + [pl.BlockSpec((SUB, LANES), lambda i, *_: (0, 0)), anywhere],
            out_specs=[block] * CORES,
            scratch_shapes=[
                pltpu.VMEM((raw_rows, LANES), F32),
                pltpu.VMEM(table.shape[1:], BF16),
                pltpu.VMEM((2, 2, GRID, LANES), F32),
                pltpu.VMEM((RADIX, 2, 2 * REST * LANES, LANES), BF16),
                pltpu.VMEM((RADIX, 2, 2 * REST * LANES, LANES), BF16),
                pltpu.VMEM((BATCH, SUB, LANES), F32),
                pltpu.VMEM((4 * BATCH, LANES), F32),
                pltpu.VMEM((16, BATCH, LANES), F32),
                pltpu.SemaphoreType.DMA((blocks,)),
                pltpu.SemaphoreType.DMA((2,)),
            ],
        ),
        out_shape=[jax.ShapeDtypeStruct((per_device, 2, columns, LANES), F32)] * CORES,
        compiler_params=pltpu.CompilerParams(
            dimension_semantics=("arbitrary",), vmem_limit_bytes=56 * 1024 * 1024
        ),
        name="spectra_rows",
    )(info, order, *raws, jnp.asarray(cot_table()), jnp.asarray(table))


def columns_kernel(info, *refs):
    pieces = refs[:CORES]
    high_hbm, low_hbm, out_hbm, out, x, high, low, piece_sem, tab_sem, out_sem = refs[CORES:]
    me = info[0]
    per_device, _, columns, _ = pieces[0].shape
    copies = [
        pltpu.make_async_copy(
            pieces[slot],
            x.at[pl.ds(((me + CORES - slot) % CORES) * per_device, per_device)],
            piece_sem.at[slot],
        )
        for slot in range(CORES)
    ]
    tab_copies = [
        pltpu.make_async_copy(high_hbm, high, tab_sem.at[0]),
        pltpu.make_async_copy(low_hbm, low, tab_sem.at[1]),
    ]
    for copy in copies + tab_copies:
        copy.start()
    for copy in copies:
        copy.wait()

    def butterflies(i, _):
        at = pl.ds(pl.multiple_of(i * 8, 8), 8)
        values = []
        for r in range(FB):
            slot = (r % CORES) * per_device + r // CORES
            values.append((x[slot, 0, at, :], x[slot, 1, at, :]))
        for r, (real, imag) in enumerate(fft_list(values)):
            x[r, 0, at, :] = real
            x[r, 1, at, :] = imag
        return 0

    lax.fori_loop(0, columns // 8, butterflies, 0)
    for copy in tab_copies:
        copy.wait()

    def transform(r):
        z_high, z_low = split(jnp.concatenate([x[r, 0], x[r, 1]], axis=1))
        f_high = high[r]
        return dot_nt(f_high, z_high) + dot_nt(low[r], z_high) + dot_nt(f_high, z_low)

    def store(i):
        at = pl.ds(pl.multiple_of(i * UNROLL, UNROLL), UNROLL)
        return [
            pltpu.make_async_copy(
                out.at[:, part, :, at, :],
                out_hbm.at[:, :, at, pl.ds(part * LANES, LANES)],
                out_sem.at[part],
            )
            for part in range(columns // LANES)
        ]

    def several(i, _):
        done = [(i * UNROLL + k, transform(i * UNROLL + k)) for k in range(UNROLL)]
        for r, y in done:
            for part in range(columns // LANES):
                for c in range(2):
                    out[c, part, :, r, :] = y[
                        c * LANES : (c + 1) * LANES, part * LANES : (part + 1) * LANES
                    ]
        @pl.when(i > 0)
        def _():
            for copy in store(i - 1):
                copy.wait()

        for copy in store(i):
            copy.start()
        return 0

    lax.fori_loop(0, FB // UNROLL, several, 0)
    for copy in store(FB // UNROLL - 1):
        copy.wait()


def column_transform(pieces, info, columns):
    high, low = column_table()
    anywhere = pl.BlockSpec(memory_space=pl.ANY)

    return pl.pallas_call(
        columns_kernel,
        grid_spec=pltpu.PrefetchScalarGridSpec(
            num_scalar_prefetch=1,
            grid=(1,),
            in_specs=[anywhere] * (CORES + 2),
            out_specs=anywhere,
            scratch_shapes=[
                pltpu.VMEM((2, columns // LANES, LANES, FB, LANES), F32),
                pltpu.VMEM((FB, 2, columns, LANES), F32),
                pltpu.VMEM(high.shape, BF16),
                pltpu.VMEM(low.shape, BF16),
                pltpu.SemaphoreType.DMA((CORES,)),
                pltpu.SemaphoreType.DMA((2,)),
                pltpu.SemaphoreType.DMA((columns // LANES,)),
            ],
        ),
        out_shape=jax.ShapeDtypeStruct((2, LANES, FB, columns), F32),
        compiler_params=pltpu.CompilerParams(vmem_limit_bytes=62 * 1024 * 1024),
        name="column_transform",
    )(info, *pieces, jnp.asarray(high), jnp.asarray(low))


def chip_cycle(chips):
    return list(range(0, chips, 2)) + list(range(chips - 1, 0, -2))[: chips // 2]


def gather_all(block, size, half):
    chips = size // CORES
    cycle = chip_cycle(chips)
    ahead, back = [], []
    for at in range(chips):
        here, there = cycle[at], cycle[(at + 1) % chips]
        for core in range(CORES):
            ahead.append((CORES * here + core, CORES * there + core))
            back.append((CORES * there + core, CORES * here + core))
    swap = [(i, i ^ 1) for i in range(size)]
    found = [[block]]
    forth = other = block
    for k in range(1, (chips + 2) // 2):
        if 2 * k == chips:
            upper = lax.ppermute(forth[:half], "wide", ahead)
            lower = lax.ppermute(other[half:], "wide", back)
            found.append([upper, lower])
        else:
            forth = lax.ppermute(forth, "wide", ahead)
            other = lax.ppermute(other, "wide", back)
            found.append([forth, other])
    swapped = []
    for some in (found[:-2], found[-2:-1], found[-1:]):
        arrays = [x for each in some for x in each]
        if arrays:
            together = jnp.concatenate(arrays, axis=0) if len(arrays) > 1 else arrays[0]
            swapped.append(lax.ppermute(together, "wide", swap))
    return [x for each in found for x in each] + swapped


def tags_of(arrays, rows, first, count):
    spots, base = [], 0
    for i, array in enumerate(arrays):
        end = base + array.shape[0]
        for at in range(-(-(base - first) // rows) * rows + first, end, rows):
            spots.append((i, at - base))
        base = end
    tag_rows = rows - first

    def kernel(*refs):
        inputs, out, sems = refs[: len(arrays)], refs[-2], refs[-1]
        copies = [
            pltpu.make_async_copy(inputs[i].at[pl.ds(at, tag_rows)], out.at[k], sems.at[k])
            for k, (i, at) in enumerate(spots)
        ]
        for copy in copies:
            copy.start()
        for copy in copies:
            copy.wait()

    tags = pl.pallas_call(
        kernel,
        in_specs=[pl.BlockSpec(memory_space=pl.ANY)] * len(arrays),
        out_specs=pl.BlockSpec(memory_space=pltpu.VMEM),
        scratch_shapes=[pltpu.SemaphoreType.DMA((len(spots),))],
        out_shape=jax.ShapeDtypeStruct((len(spots), tag_rows, LANES), F32),
        name="tags",
    )(*arrays)
    return tags.reshape(len(spots), -1)[:, :count].astype(jnp.int32)


def per_device(visibilities, offsets, vis_count, owner, tile_row, tile_col):
    size = lax.axis_size("wide")
    count, _, slots = visibilities.shape
    chips = size // CORES
    columns = GRID // size
    band_tiles = GRID // (SUB * size)
    place = lax.axis_index("wide")
    core, chip = place % CORES, place // CORES
    first = 4 * count
    rows = first + 8 * -(-count // (8 * LANES))
    bits = (size * rows // 4 - 1).bit_length()

    live = (jnp.arange(slots)[None, :] < vis_count[:, None])[:, None, :]
    items = jnp.concatenate([jnp.where(live, visibilities, 0.0), offsets], axis=1)
    tiles = ((owner * band_tiles + tile_row) * LANES + tile_col).astype(F32)
    tiles = jnp.pad(tiles, (0, (rows - first) * LANES - count)).reshape(-1, LANES)
    block = jnp.concatenate([items.reshape(first, slots), tiles], axis=0)
    gathered = gather_all(block, size, rows // 16 * 8)

    tiles = tags_of(gathered, rows, first, count)
    group, part, tile_at = tiles // (4 * LANES), tiles // LANES % 4, tiles % LANES
    key = (group % CORES) * (FB // CORES) + group // CORES
    data_at = jnp.arange(size)[:, None] * (rows // 4) + jnp.arange(count)[None, :]
    word = (((key * 4 + part) * LANES + tile_at) << bits) + data_at
    order = lax.sort(word.reshape(-1).astype(jnp.int32), is_stable=False)
    steps = FB // CORES // 2
    shift = bits + 7 + 2 + 1
    bounds = core * steps + jnp.arange(steps + 1)
    starts = jnp.sum((order[None, :] >> shift) < bounds[:, None], axis=1)
    info = jnp.concatenate([core[None], chip[None], starts]).astype(jnp.int32)

    scale = 1.0 / (math.sqrt(slots) * SUB * GRID)
    pieces = spectra_rows(gathered, info, order, chips, columns, bits, scale)
    swap = [(i, i ^ 1) for i in range(size)]
    received = [pieces[0], lax.ppermute(pieces[1], "wide", swap)]
    return column_transform(received, info, columns).reshape(2, GRID, columns)


def solution(mesh):
    placed = (
        P(("group", "wide"), None, None),
        P(("group", "wide"), None, None),
        P(("group", "wide")),
        P(("group", "wide")),
        P(("group", "wide")),
        P(("group", "wide")),
    )
    return jax.shard_map(
        per_device, mesh=mesh, in_specs=placed, out_specs=P(None, "group", "wide"), check_vma=False
    )
```

```python
import functools
import math

import jax
import jax.numpy as jnp
import ml_dtypes
import numpy as np
from jax import lax
from jax.experimental import pallas as pl
from jax.experimental.pallas import tpu as pltpu
from jax.sharding import PartitionSpec as P

SUB = 32
GRID = 4096
LANES = 128
FB = GRID // LANES
BATCH = 32
UNROLL = 8
QUARTERS = 4
RADIX = 8
REST = FB // RADIX
CORES = 2

BF16 = jnp.bfloat16
F32 = jnp.float32


def split_np(table):
    table = table.astype(np.float32)
    high = table.astype(ml_dtypes.bfloat16)
    low = (table - high.astype(np.float32)).astype(ml_dtypes.bfloat16)
    return high, low


def embed(phase):
    angle = -2.0 * np.pi * (phase % GRID) / GRID
    real, imag = np.cos(angle), np.sin(angle)
    top = np.concatenate([real, -imag], axis=-1)
    bottom = np.concatenate([imag, real], axis=-1)
    return split_np(np.concatenate([top, bottom], axis=-2))


@functools.cache
def row_table(chips):
    count = LANES // chips
    chip = np.arange(chips)[:, None, None, None, None]
    first = np.arange(RADIX)[None, :, None, None, None]
    output = np.arange(REST * count)[None, None, :, None, None] + REST * count * chip
    inner = np.arange(REST * LANES).reshape(1, 1, 1, REST, LANES)
    phase = (first + RADIX * output) * inner % GRID
    roots = np.exp(-2j * np.pi * np.arange(GRID) / GRID)
    real, imag = roots.real.astype(np.float32)[phase], roots.imag.astype(np.float32)[phase]
    top = np.stack([real, -imag], axis=4)
    bottom = np.stack([imag, real], axis=4)
    full = np.concatenate([top, bottom], axis=2)
    full = full.reshape(chips, RADIX, 2 * REST * count, -1)
    return np.concatenate(split_np(full), axis=2)


@functools.cache
def column_table():
    first = np.arange(FB)[:, None, None]
    outer = np.arange(LANES)[None, :, None]
    inner = np.arange(LANES)[None, None, :]
    return np.concatenate(embed(inner * (first + FB * outer)), axis=1)


def even_fit(function, reach, degree):
    nodes = np.cos(np.pi * (np.arange(200) + 0.5) / 200)
    points = (nodes + 1.0) / 2.0 * reach * reach
    cheb = np.polynomial.chebyshev.Chebyshev.fit(
        points, function(np.sqrt(points)), degree, domain=[0.0, reach * reach]
    )
    return [float(c) for c in cheb.convert(kind=np.polynomial.Polynomial).coef]


SIN_FIT = even_fit(lambda x: np.sin(np.pi * x) / x, 0.5, 6)
COS_FIT = even_fit(lambda x: np.cos(np.pi * x), 0.5, 7)
PEAK_FIT = even_fit(lambda x: np.sin(np.pi * x) / np.tan(np.pi * x / SUB), 0.5, 6)


def horner(coefs, x):
    total = jnp.full_like(x, coefs[-1])
    for coef in coefs[-2::-1]:
        total = total * x + coef
    return total


def cot_table():
    grid = np.arange(SUB, dtype=np.float64)
    grid[0] = 1.0
    values = 1.0 / np.tan(np.pi * grid / SUB)
    values[0] = 1e30
    return np.tile(values.astype(np.float32)[:, None], (1, LANES))


def turn(value, k, n):
    real, imag = value
    k = k % n
    if k == 0:
        return value
    if 4 * k == n:
        return (imag, -real)
    if 2 * k == n:
        return (-real, -imag)
    if 8 * k == n:
        root = math.sqrt(0.5)
        return ((real + imag) * root, (imag - real) * root)
    if 8 * k == 3 * n:
        root = math.sqrt(0.5)
        return ((imag - real) * root, (real + imag) * -root)
    cos, sin = math.cos(2.0 * math.pi * k / n), -math.sin(2.0 * math.pi * k / n)
    return (real * cos - imag * sin, real * sin + imag * cos)


def fft_list(values):
    n = len(values)
    if n == 1:
        return values
    even, odd = fft_list(values[0::2]), fft_list(values[1::2])
    first, second = [], []
    for k in range(n // 2):
        turned = turn(odd[k], k, n)
        first.append((even[k][0] + turned[0], even[k][1] + turned[1]))
        second.append((even[k][0] - turned[0], even[k][1] - turned[1]))
    return first + second


def split(x):
    high = x.astype(BF16)
    return high, (x - high.astype(F32)).astype(BF16)


def dot(a, b):
    return lax.dot_general(a, b, (((1,), (0,)), ((), ())), preferred_element_type=F32)


def dot_nt(a, b):
    return lax.dot_general(a, b, (((1,), (1,)), ((), ())), preferred_element_type=F32)


def spectra_rows_kernel(blocks, bits, scale, info, order, *refs):
    raws = refs[:blocks]
    cot_ref, table_hbm = refs[blocks : blocks + 2]
    outs = refs[blocks + 2 : blocks + 2 + CORES]
    raw, table, grid, mixed_high, mixed_low, found, rows, prep, raw_sem, tab_sem = refs[blocks + 2 + CORES :]
    step = pl.program_id(0)
    raw_copies, at = [], 0
    for i in range(blocks):
        size = raws[i].shape[0]
        raw_copies.append(pltpu.make_async_copy(raws[i], raw.at[pl.ds(at, size)], raw_sem.at[i]))
        at += size
    me = info[0]
    tab_copy = pltpu.make_async_copy(table_hbm.at[info[1]], table, tab_sem.at[0])

    @pl.when(step == 0)
    def _():
        for copy in raw_copies:
            copy.start()
        tab_copy.start()

        def clear(i, _):
            grid[:, :, pl.ds(i * 128, 128), :] = jnp.zeros((2, 2, 128, LANES), F32)
            return 0

        lax.fori_loop(0, GRID // 128, clear, 0)
        for copy in raw_copies:
            copy.wait()

    start, end = info[2 + step], info[3 + step]
    last = order.shape[0] - 1
    cell = lax.broadcasted_iota(jnp.int32, (SUB, LANES), 0).astype(F32)
    lane_part = lax.broadcasted_iota(jnp.int32, (SUB, LANES), 1) // SUB
    sub_row = lax.broadcasted_iota(jnp.int32, (BATCH, LANES), 0)

    def words_of(b):
        base = start + b * BATCH
        return [order[jnp.clip(base + j, 0, last)] for j in range(BATCH)]

    def prepare(b):
        base = start + b * BATCH
        words = words_of(b)
        for j in range(BATCH):
            item = words[j] & ((1 << bits) - 1)
            rows[4 * j : 4 * j + 4, :] = raw[pl.ds(4 * item, 4), :]
        factor = jnp.where(sub_row + base < end, scale, 0.0)
        re = rows[pl.ds(0, BATCH, stride=4), :] * factor
        im = rows[pl.ds(1, BATCH, stride=4), :] * factor
        values = {14: re, 15: im}
        for axis in range(2):
            u = rows[pl.ds(2 + axis, BATCH, stride=4), :]
            near = jnp.floor(u + 0.5)
            off = u - near
            sign = 1.0 - 2.0 * (near - 2.0 * jnp.floor(near * 0.5))
            wide = (u - SUB // 2) * (1.0 / SUB)
            wide2, off2 = wide * wide, off * off
            cot = -(wide * horner(SIN_FIT, wide2)) / horner(COS_FIT, wide2)
            sine = sign * (off * horner(SIN_FIT, off2))
            at = 8 * axis
            values[at + 0] = cot
            values[at + 1] = sine * cot
            values[at + 2] = sine * (1.0 + cot * cot)
            values[at + 3] = sign * horner(PEAK_FIT, off2)
            values[at + 4] = near
            values[at + 5] = sine
            if axis == 0:
                values[6] = im * sine
                values[7] = re * sine
        for at, value in values.items():
            prep[at] = value

    def dirichlet(axis, j):
        at = 8 * axis
        cot, alpha, beta, peak, near = [prep[at + i, j : j + 1, :] for i in range(5)]
        gap = cot_ref[...] - cot
        inv = pl.reciprocal(gap, approx=True)
        return jnp.where(cell == near, peak, alpha + beta * inv)

    def multiply():
        products = []
        for j in range(BATCH):
            table_u, table_v = dirichlet(0, j), dirichlet(1, j)
            re_j, im_j = prep[14, j : j + 1, :], prep[15, j : j + 1, :]
            b_re = re_j * table_u + prep[6, j : j + 1, :]
            b_im = im_j * table_u - prep[7, j : j + 1, :]
            sine = jnp.broadcast_to(prep[13, j : j + 1, :], (16, LANES))
            a_high, a_low = split(jnp.concatenate([table_v, sine], axis=0))
            b_high, b_low = split(jnp.concatenate([b_re, b_im], axis=0))
            product = dot_nt(
                jnp.concatenate([a_high, a_low, a_high], axis=1),
                jnp.concatenate([b_high, b_high, b_low], axis=1),
            )
            product = jnp.concatenate([product, jnp.zeros_like(product)], axis=1)
            extra = product[SUB : SUB + 8]
            extra = jnp.where(lane_part[:8] == 0, pltpu.roll(extra, 96, 1), -pltpu.roll(extra, 32, 1))
            products.append(product[:SUB] + jnp.concatenate([extra] * (SUB // 8), axis=0))
        return products

    def deposit(b):
        words = words_of(b)
        for j in range(BATCH):
            word = words[j]
            tile = (word >> bits) & (LANES - 1)
            part = (word >> (bits + 7)) & 3
            half = (word >> (bits + 9)) & 1
            mask = lane_part == part
            spot = pl.ds(pl.multiple_of(tile * SUB, SUB), SUB)
            value = found[j]
            grid[0, half, spot, :] += jnp.where(mask, pltpu.roll(value, part * SUB, 1), 0.0)
            moved = pltpu.roll(value, (part * SUB + 96) & 127, 1)
            grid[1, half, spot, :] += jnp.where(mask, moved, 0.0)

    found[...] = jnp.zeros(found.shape, F32)
    batches = (end - start + BATCH - 1) // BATCH
    prepare(0)

    def batch(b, _):
        deposit(b - 1)
        for j, product in enumerate(multiply()):
            found[j] = product
        prepare(b + 1)
        return 0

    lax.fori_loop(0, batches, batch, 0)
    deposit(batches - 1)

    @pl.when(step == 0)
    def _():
        tab_copy.wait()

    zero = jnp.zeros((16, LANES), F32)

    def butterflies(i, _):
        half, at = i % 2, pl.multiple_of(i // 2 * 16, 16)
        for b in range(REST):
            places = [
                pl.ds(pl.multiple_of((REST * a + b) * LANES + at, 16), 16) for a in range(RADIX)
            ]
            values = [tuple(grid[c, half, p, :] for c in range(2)) for p in places]
            for p in places:
                for c in range(2):
                    grid[c, half, p, :] = zero
            for r, value in enumerate(fft_list(values)):
                for c in range(2):
                    spot = pl.ds(pl.multiple_of((2 * b + c) * LANES + at, 16), 16)
                    mixed_high[r, half, spot, :], mixed_low[r, half, spot, :] = split(value[c])
        return 0

    lax.fori_loop(0, 2 * LANES // 16, butterflies, 0)

    outputs = table.shape[1] // 4
    share = outputs // CORES

    def transform(r):
        x_high = jnp.concatenate([mixed_high[r, 0], mixed_high[r, 1]], axis=1)
        x_low = jnp.concatenate([mixed_low[r, 0], mixed_low[r, 1]], axis=1)
        f = table[r]
        y = dot(f, x_high)
        return y[: 2 * outputs] + y[2 * outputs :] + dot(f[: 2 * outputs], x_low)

    def place(r, y):
        for c in range(2):
            shares = [
                y[c * outputs + k * share : c * outputs + (k + 1) * share] for k in range(CORES)
            ]
            for slot in range(CORES):
                value = shares[slot]
                for dest in range(CORES):
                    value = jnp.where((me + slot) % CORES == dest, shares[dest], value)
                for half in range(2):
                    outs[slot][half, c, pl.ds(r, share, stride=RADIX), :] = value[
                        :, half * LANES : (half + 1) * LANES
                    ]

    def several(i, _):
        done = [(4 * i + k, transform(4 * i + k)) for k in range(4)]
        for item in done:
            place(*item)
        return 0

    lax.fori_loop(0, RADIX // 4, several, 0)


def spectra_rows(raws, info, order, chips, columns, bits, scale):
    blocks = len(raws)
    table = row_table(chips)
    per_device = FB // CORES
    steps = per_device // 2
    block = pl.BlockSpec((2, 2, columns, LANES), lambda i, *_: (i, 0, 0, 0))
    anywhere = pl.BlockSpec(memory_space=pl.ANY)
    raw_rows = sum(x.shape[0] for x in raws)
    return pl.pallas_call(
        functools.partial(spectra_rows_kernel, blocks, bits, scale),
        grid_spec=pltpu.PrefetchScalarGridSpec(
            num_scalar_prefetch=2,
            grid=(steps,),
            in_specs=[anywhere] * blocks
            + [pl.BlockSpec((SUB, LANES), lambda i, *_: (0, 0)), anywhere],
            out_specs=[block] * CORES,
            scratch_shapes=[
                pltpu.VMEM((raw_rows, LANES), F32),
                pltpu.VMEM(table.shape[1:], BF16),
                pltpu.VMEM((2, 2, GRID, LANES), F32),
                pltpu.VMEM((RADIX, 2, 2 * REST * LANES, LANES), BF16),
                pltpu.VMEM((RADIX, 2, 2 * REST * LANES, LANES), BF16),
                pltpu.VMEM((BATCH, SUB, LANES), F32),
                pltpu.VMEM((4 * BATCH, LANES), F32),
                pltpu.VMEM((16, BATCH, LANES), F32),
                pltpu.SemaphoreType.DMA((blocks,)),
                pltpu.SemaphoreType.DMA((2,)),
            ],
        ),
        out_shape=[jax.ShapeDtypeStruct((per_device, 2, columns, LANES), F32)] * CORES,
        compiler_params=pltpu.CompilerParams(
            dimension_semantics=("arbitrary",), vmem_limit_bytes=56 * 1024 * 1024
        ),
        name="spectra_rows",
    )(info, order, *raws, jnp.asarray(cot_table()), jnp.asarray(table))


def columns_kernel(info, *refs):
    pieces = refs[:CORES]
    table_hbm, out_hbm, out, x, table, piece_sem, tab_sem, out_sem = refs[CORES:]
    me = info[0]
    per_device, _, columns, _ = pieces[0].shape
    quarter = columns // QUARTERS

    def fetch(i):
        at = pl.ds(pl.multiple_of(i * quarter, quarter), quarter)
        return [
            pltpu.make_async_copy(
                pieces[slot].at[:, :, at],
                x.at[pl.ds(((me + CORES - slot) % CORES) * per_device, per_device), :, at],
                piece_sem.at[slot, i],
            )
            for slot in range(CORES)
        ]

    tab_copy = pltpu.make_async_copy(table_hbm, table, tab_sem.at[0])
    for i in range(QUARTERS):
        for copy in fetch(i):
            copy.start()
    tab_copy.start()

    def butterflies(i, _):
        at = pl.ds(pl.multiple_of(i * 8, 8), 8)
        values = []
        for r in range(FB):
            slot = (r % CORES) * per_device + r // CORES
            values.append((x[slot, 0, at, :], x[slot, 1, at, :]))
        for r, (real, imag) in enumerate(fft_list(values)):
            x[r, 0, at, :] = real
            x[r, 1, at, :] = imag
        return 0

    for i in range(QUARTERS):
        for copy in fetch(i):
            copy.wait()
        lax.fori_loop(i * quarter // 8, (i + 1) * quarter // 8, butterflies, 0)
    tab_copy.wait()

    def transform(r):
        z_high, z_low = split(jnp.concatenate([x[r, 0], x[r, 1]], axis=1))
        f = table[r]
        y = dot_nt(f, z_high)
        return y[: 2 * LANES] + y[2 * LANES :] + dot_nt(f[: 2 * LANES], z_low)

    def store(i):
        at = pl.ds(pl.multiple_of(i * UNROLL, UNROLL), UNROLL)
        return [
            pltpu.make_async_copy(
                out.at[:, part, :, at, :],
                out_hbm.at[:, :, at, pl.ds(part * LANES, LANES)],
                out_sem.at[part],
            )
            for part in range(columns // LANES)
        ]

    def several(i, _):
        done = [(i * UNROLL + k, transform(i * UNROLL + k)) for k in range(UNROLL)]
        for r, y in done:
            for part in range(columns // LANES):
                for c in range(2):
                    out[c, part, :, r, :] = y[
                        c * LANES : (c + 1) * LANES, part * LANES : (part + 1) * LANES
                    ]
        @pl.when(i > 0)
        def _():
            for copy in store(i - 1):
                copy.wait()

        for copy in store(i):
            copy.start()
        return 0

    lax.fori_loop(0, FB // UNROLL, several, 0)
    for copy in store(FB // UNROLL - 1):
        copy.wait()


def column_transform(pieces, info, columns):
    table = column_table()
    anywhere = pl.BlockSpec(memory_space=pl.ANY)

    return pl.pallas_call(
        columns_kernel,
        grid_spec=pltpu.PrefetchScalarGridSpec(
            num_scalar_prefetch=1,
            grid=(1,),
            in_specs=[anywhere] * (CORES + 1),
            out_specs=anywhere,
            scratch_shapes=[
                pltpu.VMEM((2, columns // LANES, LANES, FB, LANES), F32),
                pltpu.VMEM((FB, 2, columns, LANES), F32),
                pltpu.VMEM(table.shape, BF16),
                pltpu.SemaphoreType.DMA((CORES, QUARTERS)),
                pltpu.SemaphoreType.DMA((1,)),
                pltpu.SemaphoreType.DMA((columns // LANES,)),
            ],
        ),
        out_shape=jax.ShapeDtypeStruct((2, LANES, FB, columns), F32),
        compiler_params=pltpu.CompilerParams(vmem_limit_bytes=62 * 1024 * 1024),
        name="column_transform",
    )(info, *pieces, jnp.asarray(table))


def chip_cycle(chips):
    return list(range(0, chips, 2)) + list(range(chips - 1, 0, -2))[: chips // 2]


def gather_all(block, size, half):
    chips = size // CORES
    cycle = chip_cycle(chips)
    ahead, back = [], []
    for at in range(chips):
        here, there = cycle[at], cycle[(at + 1) % chips]
        for core in range(CORES):
            ahead.append((CORES * here + core, CORES * there + core))
            back.append((CORES * there + core, CORES * here + core))
    swap = [(i, i ^ 1) for i in range(size)]
    found = [[block]]
    forth = other = block
    for k in range(1, (chips + 2) // 2):
        if 2 * k == chips:
            upper = lax.ppermute(forth[:half], "wide", ahead)
            lower = lax.ppermute(other[half:], "wide", back)
            found.append([upper, lower])
        else:
            forth = lax.ppermute(forth, "wide", ahead)
            other = lax.ppermute(other, "wide", back)
            found.append([forth, other])
    swapped = []
    for some in (found[:-2], found[-2:-1], found[-1:]):
        arrays = [x for each in some for x in each]
        if arrays:
            together = jnp.concatenate(arrays, axis=0) if len(arrays) > 1 else arrays[0]
            swapped.append(lax.ppermute(together, "wide", swap))
    return [x for each in found for x in each] + swapped


def tags_of(arrays, rows, first, count):
    spots, base = [], 0
    for i, array in enumerate(arrays):
        end = base + array.shape[0]
        for at in range(-(-(base - first) // rows) * rows + first, end, rows):
            spots.append((i, at - base))
        base = end
    tag_rows = rows - first

    def kernel(*refs):
        inputs, out, sems = refs[: len(arrays)], refs[-2], refs[-1]
        copies = [
            pltpu.make_async_copy(inputs[i].at[pl.ds(at, tag_rows)], out.at[k], sems.at[k])
            for k, (i, at) in enumerate(spots)
        ]
        for copy in copies:
            copy.start()
        for copy in copies:
            copy.wait()

    tags = pl.pallas_call(
        kernel,
        in_specs=[pl.BlockSpec(memory_space=pl.ANY)] * len(arrays),
        out_specs=pl.BlockSpec(memory_space=pltpu.VMEM),
        scratch_shapes=[pltpu.SemaphoreType.DMA((len(spots),))],
        out_shape=jax.ShapeDtypeStruct((len(spots), tag_rows, LANES), F32),
        compiler_params=pltpu.CompilerParams(vmem_limit_bytes=62 * 1024 * 1024),
        name="tags",
    )(*arrays)
    return tags.reshape(len(spots), -1)[:, :count].astype(jnp.int32)


def per_device(visibilities, offsets, vis_count, owner, tile_row, tile_col):
    size = lax.axis_size("wide")
    count, _, slots = visibilities.shape
    chips = size // CORES
    columns = GRID // size
    band_tiles = GRID // (SUB * size)
    place = lax.axis_index("wide")
    core, chip = place % CORES, place // CORES
    first = 4 * count
    rows = first + 8 * -(-count // (8 * LANES))
    bits = (size * rows // 4 - 1).bit_length()

    live = (jnp.arange(slots)[None, :] < vis_count[:, None])[:, None, :]
    items = jnp.concatenate([jnp.where(live, visibilities, 0.0), offsets], axis=1)
    tiles = ((owner * band_tiles + tile_row) * LANES + tile_col).astype(F32)
    tiles = jnp.pad(tiles, (0, (rows - first) * LANES - count)).reshape(-1, LANES)
    block = jnp.concatenate([items.reshape(first, slots), tiles], axis=0)
    gathered = gather_all(block, size, rows // 16 * 8)

    tiles = tags_of(gathered, rows, first, count)
    group, part, tile_at = tiles // (4 * LANES), tiles // LANES % 4, tiles % LANES
    key = (group % CORES) * (FB // CORES) + group // CORES
    data_at = jnp.arange(size)[:, None] * (rows // 4) + jnp.arange(count)[None, :]
    word = (((key * 4 + part) * LANES + tile_at) << bits) + data_at
    order = lax.sort(word.reshape(-1).astype(jnp.int32), is_stable=False)
    steps = FB // CORES // 2
    shift = bits + 7 + 2 + 1
    bounds = core * steps + jnp.arange(steps + 1)
    starts = jnp.sum((order[None, :] >> shift) < bounds[:, None], axis=1)
    info = jnp.concatenate([core[None], chip[None], starts]).astype(jnp.int32)

    scale = 1.0 / (math.sqrt(slots) * SUB * GRID)
    pieces = spectra_rows(gathered, info, order, chips, columns, bits, scale)
    swap = [(i, i ^ 1) for i in range(size)]
    received = [pieces[0], lax.ppermute(pieces[1], "wide", swap)]
    return column_transform(received, info, columns).reshape(2, GRID, columns)


def solution(mesh):
    placed = (
        P(("group", "wide"), None, None),
        P(("group", "wide"), None, None),
        P(("group", "wide")),
        P(("group", "wide")),
        P(("group", "wide")),
        P(("group", "wide")),
    )
    return jax.shard_map(
        per_device, mesh=mesh, in_specs=placed, out_specs=P(None, "group", "wide"), check_vma=False
    )
```

```python
import functools
import math

import jax
import jax.numpy as jnp
import ml_dtypes
import numpy as np
from jax import lax
from jax.experimental import pallas as pl
from jax.experimental.pallas import tpu as pltpu
from jax.sharding import PartitionSpec as P

SUB = 32
GRID = 4096
LANES = 128
FB = GRID // LANES
BATCH = 32
UNROLL = 8
QUARTERS = 4
RADIX = 8
REST = FB // RADIX
CORES = 2

BF16 = jnp.bfloat16
F32 = jnp.float32


def split_np(table):
    table = table.astype(np.float32)
    high = table.astype(ml_dtypes.bfloat16)
    low = (table - high.astype(np.float32)).astype(ml_dtypes.bfloat16)
    return high, low


def embed(phase):
    angle = -2.0 * np.pi * (phase % GRID) / GRID
    real, imag = np.cos(angle), np.sin(angle)
    top = np.concatenate([real, -imag], axis=-1)
    bottom = np.concatenate([imag, real], axis=-1)
    return split_np(np.concatenate([top, bottom], axis=-2))


@functools.cache
def row_table(chips):
    count = LANES // chips
    chip = np.arange(chips)[:, None, None, None, None]
    first = np.arange(RADIX)[None, :, None, None, None]
    output = np.arange(REST * count)[None, None, :, None, None] + REST * count * chip
    inner = np.arange(REST * LANES).reshape(1, 1, 1, REST, LANES)
    phase = (first + RADIX * output) * inner % GRID
    roots = np.exp(-2j * np.pi * np.arange(GRID) / GRID)
    real, imag = roots.real.astype(np.float32)[phase], roots.imag.astype(np.float32)[phase]
    top = np.stack([real, -imag], axis=4)
    bottom = np.stack([imag, real], axis=4)
    full = np.concatenate([top, bottom], axis=2)
    full = full.reshape(chips, RADIX, 2 * REST * count, -1)
    return np.concatenate(split_np(full), axis=2)


@functools.cache
def column_table():
    first = np.arange(FB)[:, None, None]
    outer = np.arange(LANES)[None, :, None]
    inner = np.arange(LANES)[None, None, :]
    return np.concatenate(embed(inner * (first + FB * outer)), axis=1)


def even_fit(function, reach, degree):
    nodes = np.cos(np.pi * (np.arange(200) + 0.5) / 200)
    points = (nodes + 1.0) / 2.0 * reach * reach
    cheb = np.polynomial.chebyshev.Chebyshev.fit(
        points, function(np.sqrt(points)), degree, domain=[0.0, reach * reach]
    )
    return [float(c) for c in cheb.convert(kind=np.polynomial.Polynomial).coef]


SIN_FIT = even_fit(lambda x: np.sin(np.pi * x) / x, 0.5, 6)
COS_FIT = even_fit(lambda x: np.cos(np.pi * x), 0.5, 7)
PEAK_FIT = even_fit(lambda x: np.sin(np.pi * x) / np.tan(np.pi * x / SUB), 0.5, 6)


def horner(coefs, x):
    total = jnp.full_like(x, coefs[-1])
    for coef in coefs[-2::-1]:
        total = total * x + coef
    return total


def cot_table():
    grid = np.arange(SUB, dtype=np.float64)
    grid[0] = 1.0
    values = 1.0 / np.tan(np.pi * grid / SUB)
    values[0] = 1e30
    return np.tile(values.astype(np.float32)[:, None], (1, LANES))


def turn(value, k, n):
    real, imag = value
    k = k % n
    if k == 0:
        return value
    if 4 * k == n:
        return (imag, -real)
    if 2 * k == n:
        return (-real, -imag)
    if 8 * k == n:
        root = math.sqrt(0.5)
        return ((real + imag) * root, (imag - real) * root)
    if 8 * k == 3 * n:
        root = math.sqrt(0.5)
        return ((imag - real) * root, (real + imag) * -root)
    cos, sin = math.cos(2.0 * math.pi * k / n), -math.sin(2.0 * math.pi * k / n)
    return (real * cos - imag * sin, real * sin + imag * cos)


def fft_list(values):
    n = len(values)
    if n == 1:
        return values
    even, odd = fft_list(values[0::2]), fft_list(values[1::2])
    first, second = [], []
    for k in range(n // 2):
        turned = turn(odd[k], k, n)
        first.append((even[k][0] + turned[0], even[k][1] + turned[1]))
        second.append((even[k][0] - turned[0], even[k][1] - turned[1]))
    return first + second


def split(x):
    high = x.astype(BF16)
    return high, (x - high.astype(F32)).astype(BF16)


def dot(a, b):
    return lax.dot_general(a, b, (((1,), (0,)), ((), ())), preferred_element_type=F32)


def dot_nt(a, b):
    return lax.dot_general(a, b, (((1,), (1,)), ((), ())), preferred_element_type=F32)


def spectra_rows_kernel(blocks, bits, scale, info, order, *refs):
    raws = refs[:blocks]
    cot_ref, table_hbm = refs[blocks : blocks + 2]
    outs = refs[blocks + 2 : blocks + 2 + CORES]
    raw, table, grid, mixed_high, mixed_low, found, rows, prep, raw_sem, tab_sem = refs[blocks + 2 + CORES :]
    step = pl.program_id(0)
    raw_copies, at = [], 0
    for i in range(blocks):
        size = raws[i].shape[0]
        raw_copies.append(pltpu.make_async_copy(raws[i], raw.at[pl.ds(at, size)], raw_sem.at[i]))
        at += size
    me = info[0]
    tab_copy = pltpu.make_async_copy(table_hbm.at[info[1]], table, tab_sem.at[0])

    @pl.when(step == 0)
    def _():
        for copy in raw_copies:
            copy.start()
        tab_copy.start()

        def clear(i, _):
            grid[:, :, pl.ds(i * 128, 128), :] = jnp.zeros((2, 2, 128, LANES), F32)
            return 0

        lax.fori_loop(0, GRID // 128, clear, 0)
        for copy in raw_copies:
            copy.wait()

    start, end = info[2 + step], info[3 + step]
    last = order.shape[0] - 1
    cell = lax.broadcasted_iota(jnp.int32, (SUB, LANES), 0).astype(F32)
    lane_part = lax.broadcasted_iota(jnp.int32, (SUB, LANES), 1) // SUB
    sub_row = lax.broadcasted_iota(jnp.int32, (BATCH, LANES), 0)

    def words_of(b):
        base = start + b * BATCH
        return [order[jnp.clip(base + j, 0, last)] for j in range(BATCH)]

    def prepare(b):
        base = start + b * BATCH
        words = words_of(b)
        for j in range(BATCH):
            item = words[j] & ((1 << bits) - 1)
            rows[4 * j : 4 * j + 4, :] = raw[pl.ds(4 * item, 4), :]
        factor = jnp.where(sub_row + base < end, scale, 0.0)
        re = rows[pl.ds(0, BATCH, stride=4), :] * factor
        im = rows[pl.ds(1, BATCH, stride=4), :] * factor
        values = {14: re, 15: im}
        for axis in range(2):
            u = rows[pl.ds(2 + axis, BATCH, stride=4), :]
            near = jnp.floor(u + 0.5)
            off = u - near
            sign = 1.0 - 2.0 * (near - 2.0 * jnp.floor(near * 0.5))
            wide = (u - SUB // 2) * (1.0 / SUB)
            wide2, off2 = wide * wide, off * off
            cot = -(wide * horner(SIN_FIT, wide2)) / horner(COS_FIT, wide2)
            sine = sign * (off * horner(SIN_FIT, off2))
            at = 8 * axis
            values[at + 0] = cot
            values[at + 1] = sine * cot
            values[at + 2] = sine * (1.0 + cot * cot)
            values[at + 3] = sign * horner(PEAK_FIT, off2)
            values[at + 4] = near
            values[at + 5] = sine
            if axis == 0:
                values[6] = im * sine
                values[7] = re * sine
        for at, value in values.items():
            prep[at] = value

    def dirichlet(axis, j):
        at = 8 * axis
        cot, alpha, beta, peak, near = [prep[at + i, j : j + 1, :] for i in range(5)]
        gap = cot_ref[...] - cot
        inv = pl.reciprocal(gap, approx=True)
        return jnp.where(cell == near, peak, alpha + beta * inv)

    def multiply():
        products = []
        for j in range(BATCH):
            table_u, table_v = dirichlet(0, j), dirichlet(1, j)
            re_j, im_j = prep[14, j : j + 1, :], prep[15, j : j + 1, :]
            b_re = re_j * table_u + prep[6, j : j + 1, :]
            b_im = im_j * table_u - prep[7, j : j + 1, :]
            sine = jnp.broadcast_to(prep[13, j : j + 1, :], (16, LANES))
            a_high, a_low = split(jnp.concatenate([table_v, sine], axis=0))
            b_high, b_low = split(jnp.concatenate([b_re, b_im], axis=0))
            product = dot_nt(
                jnp.concatenate([a_high, a_low, a_high], axis=1),
                jnp.concatenate([b_high, b_high, b_low], axis=1),
            )
            product = jnp.concatenate([product, jnp.zeros_like(product)], axis=1)
            extra = product[SUB : SUB + 8]
            extra = jnp.where(lane_part[:8] == 0, pltpu.roll(extra, 96, 1), -pltpu.roll(extra, 32, 1))
            products.append(product[:SUB] + jnp.concatenate([extra] * (SUB // 8), axis=0))
        return products

    def deposit(b):
        words = words_of(b)
        for j in range(BATCH):
            word = words[j]
            tile = (word >> bits) & (LANES - 1)
            part = (word >> (bits + 7)) & 3
            half = (word >> (bits + 9)) & 1
            mask = lane_part == part
            spot = pl.ds(pl.multiple_of(tile * SUB, SUB), SUB)
            value = found[j]
            grid[0, half, spot, :] += jnp.where(mask, pltpu.roll(value, part * SUB, 1), 0.0)
            moved = pltpu.roll(value, (part * SUB + 96) & 127, 1)
            grid[1, half, spot, :] += jnp.where(mask, moved, 0.0)

    found[...] = jnp.zeros(found.shape, F32)
    batches = (end - start + BATCH - 1) // BATCH
    prepare(0)

    def batch(b, _):
        deposit(b - 1)
        for j, product in enumerate(multiply()):
            found[j] = product
        prepare(b + 1)
        return 0

    lax.fori_loop(0, batches, batch, 0)
    deposit(batches - 1)

    @pl.when(step == 0)
    def _():
        tab_copy.wait()

    zero = jnp.zeros((16, LANES), F32)

    def butterflies(i, _):
        half, at = i % 2, pl.multiple_of(i // 2 * 16, 16)
        for b in range(REST):
            places = [
                pl.ds(pl.multiple_of((REST * a + b) * LANES + at, 16), 16) for a in range(RADIX)
            ]
            values = [tuple(grid[c, half, p, :] for c in range(2)) for p in places]
            for p in places:
                for c in range(2):
                    grid[c, half, p, :] = zero
            for r, value in enumerate(fft_list(values)):
                for c in range(2):
                    spot = pl.ds(pl.multiple_of((2 * b + c) * LANES + at, 16), 16)
                    mixed_high[r, half, spot, :], mixed_low[r, half, spot, :] = split(value[c])
        return 0

    lax.fori_loop(0, 2 * LANES // 16, butterflies, 0)

    outputs = table.shape[1] // 4
    share = outputs // CORES

    def transform(r):
        x_high = jnp.concatenate([mixed_high[r, 0], mixed_high[r, 1]], axis=1)
        x_low = jnp.concatenate([mixed_low[r, 0], mixed_low[r, 1]], axis=1)
        f = table[r]
        y = dot(f, x_high)
        return y[: 2 * outputs] + y[2 * outputs :] + dot(f[: 2 * outputs], x_low)

    def place(r, y):
        for c in range(2):
            shares = [
                y[c * outputs + k * share : c * outputs + (k + 1) * share] for k in range(CORES)
            ]
            for slot in range(CORES):
                value = shares[slot]
                for dest in range(CORES):
                    value = jnp.where((me + slot) % CORES == dest, shares[dest], value)
                for half in range(2):
                    outs[slot][half, c, pl.ds(r, share, stride=RADIX), :] = value[
                        :, half * LANES : (half + 1) * LANES
                    ]

    def several(i, _):
        done = [(4 * i + k, transform(4 * i + k)) for k in range(4)]
        for item in done:
            place(*item)
        return 0

    lax.fori_loop(0, RADIX // 4, several, 0)


def spectra_rows(raws, info, order, chips, columns, bits, scale):
    blocks = len(raws)
    table = row_table(chips)
    per_device = FB // CORES
    steps = per_device // 2
    block = pl.BlockSpec((2, 2, columns, LANES), lambda i, *_: (i, 0, 0, 0))
    anywhere = pl.BlockSpec(memory_space=pl.ANY)
    raw_rows = sum(x.shape[0] for x in raws)
    return pl.pallas_call(
        functools.partial(spectra_rows_kernel, blocks, bits, scale),
        grid_spec=pltpu.PrefetchScalarGridSpec(
            num_scalar_prefetch=2,
            grid=(steps,),
            in_specs=[anywhere] * blocks
            + [pl.BlockSpec((SUB, LANES), lambda i, *_: (0, 0)), anywhere],
            out_specs=[block] * CORES,
            scratch_shapes=[
                pltpu.VMEM((raw_rows, LANES), F32),
                pltpu.VMEM(table.shape[1:], BF16),
                pltpu.VMEM((2, 2, GRID, LANES), F32),
                pltpu.VMEM((RADIX, 2, 2 * REST * LANES, LANES), BF16),
                pltpu.VMEM((RADIX, 2, 2 * REST * LANES, LANES), BF16),
                pltpu.VMEM((BATCH, SUB, LANES), F32),
                pltpu.VMEM((4 * BATCH, LANES), F32),
                pltpu.VMEM((16, BATCH, LANES), F32),
                pltpu.SemaphoreType.DMA((blocks,)),
                pltpu.SemaphoreType.DMA((2,)),
            ],
        ),
        out_shape=[jax.ShapeDtypeStruct((per_device, 2, columns, LANES), F32)] * CORES,
        compiler_params=pltpu.CompilerParams(
            dimension_semantics=("arbitrary",), vmem_limit_bytes=56 * 1024 * 1024
        ),
        name="spectra_rows",
    )(info, order, *raws, jnp.asarray(cot_table()), jnp.asarray(table))


def columns_kernel(info, *refs):
    pieces = refs[:CORES]
    table_hbm, out_hbm, out, x, table, piece_sem, tab_sem, out_sem = refs[CORES:]
    me = info[0]
    per_device, _, columns, _ = pieces[0].shape
    quarter = columns // QUARTERS

    def fetch(i):
        at = pl.ds(pl.multiple_of(i * quarter, quarter), quarter)
        return [
            pltpu.make_async_copy(
                pieces[slot].at[:, :, at],
                x.at[pl.ds(((me + CORES - slot) % CORES) * per_device, per_device), :, at],
                piece_sem.at[slot, i],
            )
            for slot in range(CORES)
        ]

    tab_copy = pltpu.make_async_copy(table_hbm, table, tab_sem.at[0])
    for i in range(QUARTERS):
        for copy in fetch(i):
            copy.start()
    tab_copy.start()

    def butterflies(i, _):
        at = pl.ds(pl.multiple_of(i * 8, 8), 8)
        values = []
        for r in range(FB):
            slot = (r % CORES) * per_device + r // CORES
            values.append((x[slot, 0, at, :], x[slot, 1, at, :]))
        for r, (real, imag) in enumerate(fft_list(values)):
            x[r, 0, at, :] = real
            x[r, 1, at, :] = imag
        return 0

    for i in range(QUARTERS):
        for copy in fetch(i):
            copy.wait()
        lax.fori_loop(i * quarter // 8, (i + 1) * quarter // 8, butterflies, 0)
    tab_copy.wait()

    def transform(r):
        z_high, z_low = split(jnp.concatenate([x[r, 0], x[r, 1]], axis=1))
        f = table[r]
        y = dot_nt(f, z_high)
        return y[: 2 * LANES] + y[2 * LANES :] + dot_nt(f[: 2 * LANES], z_low)

    def store(i):
        at = pl.ds(pl.multiple_of(i * UNROLL, UNROLL), UNROLL)
        return [
            pltpu.make_async_copy(
                out.at[:, part, :, at, :],
                out_hbm.at[:, :, at, pl.ds(part * LANES, LANES)],
                out_sem.at[part],
            )
            for part in range(columns // LANES)
        ]

    def several(i, _):
        done = [(i * UNROLL + k, transform(i * UNROLL + k)) for k in range(UNROLL)]
        for r, y in done:
            for part in range(columns // LANES):
                for c in range(2):
                    out[c, part, :, r, :] = y[
                        c * LANES : (c + 1) * LANES, part * LANES : (part + 1) * LANES
                    ]
        @pl.when(i > 0)
        def _():
            for copy in store(i - 1):
                copy.wait()

        for copy in store(i):
            copy.start()
        return 0

    lax.fori_loop(0, FB // UNROLL, several, 0)
    for copy in store(FB // UNROLL - 1):
        copy.wait()


def column_transform(pieces, info, columns):
    table = column_table()
    anywhere = pl.BlockSpec(memory_space=pl.ANY)

    return pl.pallas_call(
        columns_kernel,
        grid_spec=pltpu.PrefetchScalarGridSpec(
            num_scalar_prefetch=1,
            grid=(1,),
            in_specs=[anywhere] * (CORES + 1),
            out_specs=anywhere,
            scratch_shapes=[
                pltpu.VMEM((2, columns // LANES, LANES, FB, LANES), F32),
                pltpu.VMEM((FB, 2, columns, LANES), F32),
                pltpu.VMEM(table.shape, BF16),
                pltpu.SemaphoreType.DMA((CORES, QUARTERS)),
                pltpu.SemaphoreType.DMA((1,)),
                pltpu.SemaphoreType.DMA((columns // LANES,)),
            ],
        ),
        out_shape=jax.ShapeDtypeStruct((2, LANES, FB, columns), F32),
        compiler_params=pltpu.CompilerParams(vmem_limit_bytes=62 * 1024 * 1024),
        name="column_transform",
    )(info, *pieces, jnp.asarray(table))


def chip_cycle(chips):
    return list(range(0, chips, 2)) + list(range(chips - 1, 0, -2))[: chips // 2]


def gather_all(block, size, half):
    chips = size // CORES
    cycle = chip_cycle(chips)
    ahead, back = [], []
    for at in range(chips):
        here, there = cycle[at], cycle[(at + 1) % chips]
        for core in range(CORES):
            ahead.append((CORES * here + core, CORES * there + core))
            back.append((CORES * there + core, CORES * here + core))
    swap = [(i, i ^ 1) for i in range(size)]
    found = [[block]]
    forth = other = block
    for k in range(1, (chips + 2) // 2):
        if 2 * k == chips:
            upper = lax.ppermute(forth[:half], "wide", ahead)
            lower = lax.ppermute(other[half:], "wide", back)
            found.append([upper, lower])
        else:
            forth = lax.ppermute(forth, "wide", ahead)
            other = lax.ppermute(other, "wide", back)
            found.append([forth, other])
    swapped = []
    for some in (found[:-1], found[-1:]):
        arrays = [x for each in some for x in each]
        if arrays:
            together = jnp.concatenate(arrays, axis=0) if len(arrays) > 1 else arrays[0]
            swapped.append(lax.ppermute(together, "wide", swap))
    return [x for each in found for x in each] + swapped


def tags_of(arrays, rows, first, count):
    spots, base = [], 0
    for i, array in enumerate(arrays):
        end = base + array.shape[0]
        for at in range(-(-(base - first) // rows) * rows + first, end, rows):
            spots.append((i, at - base))
        base = end
    tag_rows = rows - first

    def kernel(*refs):
        inputs, out, sems = refs[: len(arrays)], refs[-2], refs[-1]
        copies = [
            pltpu.make_async_copy(inputs[i].at[pl.ds(at, tag_rows)], out.at[k], sems.at[k])
            for k, (i, at) in enumerate(spots)
        ]
        for copy in copies:
            copy.start()
        for copy in copies:
            copy.wait()

    tags = pl.pallas_call(
        kernel,
        in_specs=[pl.BlockSpec(memory_space=pl.ANY)] * len(arrays),
        out_specs=pl.BlockSpec(memory_space=pltpu.VMEM),
        scratch_shapes=[pltpu.SemaphoreType.DMA((len(spots),))],
        out_shape=jax.ShapeDtypeStruct((len(spots), tag_rows, LANES), F32),
        compiler_params=pltpu.CompilerParams(vmem_limit_bytes=62 * 1024 * 1024),
        name="tags",
    )(*arrays)
    return tags.reshape(len(spots), -1)[:, :count].astype(jnp.int32)


def per_device(visibilities, offsets, vis_count, owner, tile_row, tile_col):
    size = lax.axis_size("wide")
    count, _, slots = visibilities.shape
    chips = size // CORES
    columns = GRID // size
    band_tiles = GRID // (SUB * size)
    place = lax.axis_index("wide")
    core, chip = place % CORES, place // CORES
    first = 4 * count
    rows = first + 8 * -(-count // (8 * LANES))
    bits = (size * rows // 4 - 1).bit_length()

    live = (jnp.arange(slots)[None, :] < vis_count[:, None])[:, None, :]
    items = jnp.concatenate([jnp.where(live, visibilities, 0.0), offsets], axis=1)
    tiles = ((owner * band_tiles + tile_row) * LANES + tile_col).astype(F32)
    tiles = jnp.pad(tiles, (0, (rows - first) * LANES - count)).reshape(-1, LANES)
    block = jnp.concatenate([items.reshape(first, slots), tiles], axis=0)
    gathered = gather_all(block, size, rows // 16 * 8)

    tiles = tags_of(gathered, rows, first, count)
    group, part, tile_at = tiles // (4 * LANES), tiles // LANES % 4, tiles % LANES
    key = (group % CORES) * (FB // CORES) + group // CORES
    data_at = jnp.arange(size)[:, None] * (rows // 4) + jnp.arange(count)[None, :]
    word = (((key * 4 + part) * LANES + tile_at) << bits) + data_at
    order = lax.sort(word.reshape(-1).astype(jnp.int32), is_stable=False)
    steps = FB // CORES // 2
    shift = bits + 7 + 2 + 1
    bounds = core * steps + jnp.arange(steps + 1)
    starts = jnp.sum((order[None, :] >> shift) < bounds[:, None], axis=1)
    info = jnp.concatenate([core[None], chip[None], starts]).astype(jnp.int32)

    scale = 1.0 / (math.sqrt(slots) * SUB * GRID)
    pieces = spectra_rows(gathered, info, order, chips, columns, bits, scale)
    swap = [(i, i ^ 1) for i in range(size)]
    received = [pieces[0], lax.ppermute(pieces[1], "wide", swap)]
    return column_transform(received, info, columns).reshape(2, GRID, columns)


def solution(mesh):
    placed = (
        P(("group", "wide"), None, None),
        P(("group", "wide"), None, None),
        P(("group", "wide")),
        P(("group", "wide")),
        P(("group", "wide")),
        P(("group", "wide")),
    )
    return jax.shard_map(
        per_device, mesh=mesh, in_specs=placed, out_specs=P(None, "group", "wide"), check_vma=False
    )
```
